512 devices in a mesh: rep: 8 (over z_hi, x), seq: 64 (over z_lo, y, core).
Axes of the slice: x: 4, y: 8, z: 8 (z_hi: 2, z_lo: 4; z = z_hi * 4 + z_lo), core: 2. Of those that a mesh axis runs over, the one named last changes fastest.
Arguments:
- queries: bfloat16 [8, 8192, 4096], P('rep', 'seq'), may hold values from -6 to 6
- keys: bfloat16 [8, 8192, 512], P('rep', 'seq'), may hold values from -6 to 6
- values: bfloat16 [8, 8192, 512], P('rep', 'seq'), may hold values from -6 to 6
- doc_ids: int32 [8, 8192], P('rep', 'seq'), may hold values from 0 to 63, never falling along the last dimension, each value on 1 to 256 neighbouring positions
- coeffs: bfloat16 [8, 8192, 256], P('rep', 'seq'), may hold values from -6 to 6
- shard_dest: int32 [8, 64], P('rep', 'seq'), may hold values from 0 to 63, each once within a row
- basis: bfloat16 [256, 8192], P(None, 'seq'), may hold values from -0.0625 to 0.0625
Outputs:
- attended: bfloat16 [8, 8192, 4096], P('rep', 'seq')
- grad_proj: float32 [4096, 256], P('seq')
The draws below stay inside these ranges and needn't reach their ends.
Inputs may be any that keep to these rules, and one draw needn't show every extreme that they name: Each replica's row holds every number once; sender j of seq holds the coefficients of sequence block shard_dest[r, j]. `doc_ids`: never falling along a sequence; each document has at most 256 tokens, and one has exactly 256.
All inputs are finite; a program needn't handle non-finite values.
Results may differ from the reference program's by a relative error of at most 0.0056.
Values may be sent and summed in bfloat16 or wider, within the bound.
No kernel may reach another device: no remote copies, remote signals or barrier semaphores. Data moves between devices by JAX's collectives and lax.ppermute only.
A program may use at most 64 MiB of HBM per device.

```python
import math
import jax
import jax.numpy as jnp
import numpy as np
from jax import lax

D = 8192
R = 256
QUERY_HEADS = 32
KEY_VALUE_HEADS = 4
HEAD_SIZE = 128
BLOCK_TOKENS = 128
EARLIER_BLOCKS = 2
SEQUENCE_TOKENS = 8192
MOST = 256
N_REP = 8
N_SEQ = 64


def shared_fields(key):
    head_group = QUERY_HEADS // KEY_VALUE_HEADS
    key_layout_shape = (N_REP, SEQUENCE_TOKENS, KEY_VALUE_HEADS, HEAD_SIZE)
    query_layout_shape = (N_REP, SEQUENCE_TOKENS, KEY_VALUE_HEADS, head_group, HEAD_SIZE)
    key_outputs = jnp.clip(jax.random.normal(jax.random.fold_in(key, 11), key_layout_shape), -4.0, 4.0)
    query_outputs = jnp.clip(jax.random.normal(jax.random.fold_in(key, 12), query_layout_shape), -4.0, 4.0)
    return (key_outputs.reshape(N_REP, SEQUENCE_TOKENS, KEY_VALUE_HEADS * HEAD_SIZE), query_outputs.reshape(N_REP, SEQUENCE_TOKENS, QUERY_HEADS * HEAD_SIZE))


def draw_queries(key, part):
    return shared_fields(key)[1].astype(jnp.bfloat16)


def draw_keys(key, part):
    return shared_fields(key)[0].astype(jnp.bfloat16)


def block_levels(rng, dims, split, low, top_value):
    loudness, own = 1.0, jax.random.fold_in(rng, 6)
    for dim, parts in split:
        heights = jnp.exp(jax.random.uniform(jax.random.fold_in(own, dim), (parts,), jnp.float32, low / len(split), top_value / len(split)))
        loudness = loudness * jnp.repeat(heights, dims[dim] // parts).reshape([-1 if axis == dim else 1 for axis in range(len(dims))])
    return loudness


def profile(number_of, total, most, lean):
    loads = [(1 << 20) // math.isqrt(standing ** lean) + 1 for standing in range(2, number_of + 1)]
    surplus, given = total - most - (number_of - 1), [1] * (number_of - 1)
    while surplus > 0:
        candidates = [i for i in range(number_of - 1) if given[i] < most]
        pool, left = sum([loads[i] for i in candidates]), surplus
        for i in candidates:
            more = min(most - given[i], max(1, left * loads[i] // pool), surplus)
            given[i] = given[i] + more
            surplus = surplus - more
    return np.array([most] + given)


def ragged(own_key, number_of, total, limit, slope):
    if number_of == 2:
        one = jax.random.randint(own_key, (), max(1, total - limit), min(limit, total - 1) + 1)
        return jnp.stack([one, total - one])
    lengths = jnp.asarray(profile(number_of, total, limit, slope), jnp.int32)
    pairs = (number_of - 1) // 2
    donor, taker = lengths[1:1 + 2 * pairs:2], lengths[2:2 + 2 * pairs:2]
    slack = jnp.minimum(donor - 1, limit - taker)
    shifted = jax.random.randint(jax.random.fold_in(own_key, 1), (pairs,), 0, 1 << 20) % (slack + 1)
    lengths = lengths.at[1:1 + 2 * pairs:2].set(donor - shifted).at[2:2 + 2 * pairs:2].set(taker + shifted)
    return lengths[jax.random.permutation(jax.random.fold_in(own_key, 2), number_of)]


def normal_values(own_key, dims, scale, reach, split=(), kind=jnp.bfloat16):
    drawn = scale * jax.random.normal(own_key, dims, jnp.float32)
    if split:
        drawn = drawn * block_levels(own_key, dims, split, -0.22, 0.18)
    return jnp.clip(drawn, -reach, reach).astype(kind)


def setup_inputs(seed: int = 0) -> dict:
    key_of = jax.random.split(jax.random.key(seed), 8)
    return {
        "queries": draw_queries(jax.random.fold_in(key_of[7], 71), 0),
        "keys": draw_keys(jax.random.fold_in(key_of[7], 71), 0),
        "values": normal_values(key_of[2], (N_REP, SEQUENCE_TOKENS, KEY_VALUE_HEADS * HEAD_SIZE), 1.0, 6.0, ((0, 8), (1, 64))),
        "doc_ids": jax.vmap(lambda own: jnp.searchsorted(jnp.cumsum(ragged(own, N_SEQ, SEQUENCE_TOKENS, MOST, 2)), jnp.arange(SEQUENCE_TOKENS), side="right"))(jax.random.split(key_of[3], N_REP)).reshape((N_REP, SEQUENCE_TOKENS)).astype(jnp.int32),
        "coeffs": normal_values(key_of[4], (N_REP, SEQUENCE_TOKENS, R), 1.0, 6.0, ((0, 8), (1, 64))),
        "shard_dest": jax.vmap(lambda own: jax.random.permutation(own, N_SEQ))(jax.random.split(key_of[5], N_REP)).reshape((N_REP, N_SEQ)).astype(jnp.int32),
        "basis": normal_values(key_of[6], (R, D), D ** -0.5, 0.0625, ((1, 64),)),
    }


def attend_block(query_row_block, key_row_block, value_row_block, visible):
    token_count = query_row_block.shape[0]
    grouped_heads = query_row_block.astype(jnp.float32).reshape(token_count, KEY_VALUE_HEADS, QUERY_HEADS // KEY_VALUE_HEADS, HEAD_SIZE)
    key_tensor = key_row_block.astype(jnp.float32).reshape(-1, KEY_VALUE_HEADS, HEAD_SIZE)
    value_tensor = value_row_block.astype(jnp.float32).reshape(-1, KEY_VALUE_HEADS, HEAD_SIZE)
    scores = jnp.einsum('tkgd,skd->kgts', grouped_heads, key_tensor) * HEAD_SIZE ** (-0.5)
    scores = jnp.where(visible[None, None], scores, jnp.float32(-1e+30))
    highest = lax.optimization_barrier(jnp.max(scores, axis=-1, keepdims=True))
    expos = jnp.exp(scores - highest)
    totals = lax.optimization_barrier(jnp.sum(expos, axis=-1, keepdims=True))
    weights = (expos / totals).astype(jnp.bfloat16)
    mixed = jnp.einsum('kgts,skd->tkgd', weights.astype(jnp.float32), value_tensor)
    return mixed.reshape(token_count, QUERY_HEADS * HEAD_SIZE).astype(jnp.bfloat16)

def reference(queries, keys, values, doc_ids, coeffs, shard_dest, basis):
    window = (EARLIER_BLOCKS + 1) * BLOCK_TOKENS
    outputs = []
    gradient = jnp.zeros((QUERY_HEADS * HEAD_SIZE, R), jnp.float32)
    basis_wide = basis.astype(jnp.float32)
    for repeat_index in range(N_REP):
        key_padding = jnp.concatenate([jnp.zeros((EARLIER_BLOCKS * BLOCK_TOKENS, KEY_VALUE_HEADS * HEAD_SIZE), jnp.bfloat16), keys[repeat_index]], axis=0)
        value_padding = jnp.concatenate([jnp.zeros((EARLIER_BLOCKS * BLOCK_TOKENS, KEY_VALUE_HEADS * HEAD_SIZE), jnp.bfloat16), values[repeat_index]], axis=0)
        doc_pad = jnp.concatenate([jnp.full((EARLIER_BLOCKS * BLOCK_TOKENS,), -1, jnp.int32), doc_ids[repeat_index].astype(jnp.int32)], axis=0)
        query_all = queries[repeat_index]
        doc_all = doc_ids[repeat_index].astype(jnp.int32)

        def one_block(block):
            begin = (block * BLOCK_TOKENS).astype(jnp.int32)
            query_row_block = lax.dynamic_slice_in_dim(query_all, begin, BLOCK_TOKENS, 0)
            query_docs = lax.dynamic_slice_in_dim(doc_all, begin, BLOCK_TOKENS, 0)
            key_row_block = lax.dynamic_slice_in_dim(key_padding, begin, window, 0)
            value_row_block = lax.dynamic_slice_in_dim(value_padding, begin, window, 0)
            key_docs = lax.dynamic_slice_in_dim(doc_pad, begin, window, 0)
            query_pos = jnp.arange(BLOCK_TOKENS, dtype=jnp.int32) + EARLIER_BLOCKS * BLOCK_TOKENS
            key_pos = jnp.arange(window, dtype=jnp.int32)
            visible = (key_docs[None, :] == query_docs[:, None]) & (key_pos[None, :] <= query_pos[:, None])
            return attend_block(query_row_block, key_row_block, value_row_block, visible)
        blocks_out = lax.map(one_block, jnp.arange(N_SEQ, dtype=jnp.int32))
        attended_rep = blocks_out.reshape(SEQUENCE_TOKENS, QUERY_HEADS * HEAD_SIZE)
        outputs.append(attended_rep)
        sources = jnp.zeros((N_SEQ,), jnp.int32).at[shard_dest[repeat_index].astype(jnp.int32)].set(jnp.arange(N_SEQ, dtype=jnp.int32))
        ordered = coeffs[repeat_index].reshape(N_SEQ, BLOCK_TOKENS, R)[sources].reshape(SEQUENCE_TOKENS, R)
        rebuilt = jnp.dot(ordered, basis, preferred_element_type=jnp.float32)
        projected = jnp.dot(rebuilt, basis_wide.T, precision=lax.Precision.HIGHEST).astype(jnp.bfloat16)
        gradient = gradient + lax.dot_general(attended_rep, projected, (((0,), (0,)), ((), ())), preferred_element_type=jnp.float32)
    attended = jnp.stack(outputs, axis=0)
    grad_proj = gradient * (1.0 / math.sqrt(N_REP * SEQUENCE_TOKENS))
    return (attended, grad_proj)
```

```python
import functools
import math

import jax
import jax.numpy as jnp
from jax import lax
from jax.experimental import pallas as pl
from jax.experimental.pallas import tpu as pltpu
from jax.sharding import PartitionSpec as P

QUERY_HEADS = 32
KEY_VALUE_HEADS = 4
HEAD_SIZE = 128
GROUP = QUERY_HEADS // KEY_VALUE_HEADS
TOKENS = 128
R = 256
SEQ = 64
REP = 8
CHIPS = SEQ // 2
HALF = HEAD_SIZE // 2
LOG2E = math.log2(math.e)
VMEM_LIMIT = 48 * 1024 * 1024


def shifted(block, distance):
    return lax.ppermute(block, "seq", [(i, i + distance) for i in range(SEQ - distance)])


def other_core(block):
    return lax.ppermute(block, "seq", [(i, i ^ 1) for i in range(SEQ)])


NT = (((1,), (1,)), ((), ()))


def attention_kernel(core_ref, q_ref, own_ref, one_ref, two_ref, tags_ref, out_ref, keep_ref, send_ref):
    core = core_ref[0]
    tags = tags_ref[...]
    query_tags = jnp.broadcast_to(tags[2:3, :], (TOKENS, TOKENS))
    key_pos = lax.broadcasted_iota(jnp.int32, (TOKENS, TOKENS), 0)
    query_pos = lax.broadcasted_iota(jnp.int32, (TOKENS, TOKENS), 1)
    visible = []
    for i in range(3):
        key_tags = jnp.broadcast_to(tags[i : i + 1, :], (TOKENS, TOKENS)).T
        seen = key_tags == query_tags
        if i == 2:
            seen = seen & (key_pos <= query_pos)
        visible.append(seen)
    factor = HEAD_SIZE ** (-0.5) * LOG2E
    blocks = (two_ref, one_ref, own_ref)
    for g in range(KEY_VALUE_HEADS):
        at = g * HEAD_SIZE
        keys = [b[:, at : at + HEAD_SIZE] for b in blocks]
        values = [
            b[:, 512 + at : 512 + at + HEAD_SIZE].astype(jnp.float32).T.astype(jnp.bfloat16)
            for b in blocks
        ]
        values = jnp.concatenate(values, axis=1)
        for j in range(GROUP):
            h = g * GROUP + j
            q = q_ref[:, h * HEAD_SIZE : (h + 1) * HEAD_SIZE]
            scores = [
                jnp.where(
                    visible[i],
                    lax.dot_general(keys[i], q, NT, preferred_element_type=jnp.float32),
                    jnp.float32(-1e30),
                )
                for i in range(3)
            ]
            highest = jnp.max(
                jnp.maximum(jnp.maximum(scores[0], scores[1]), scores[2]), axis=0, keepdims=True
            )
            expos = [jnp.exp2((s - highest) * factor) for s in scores]
            totals = jnp.sum(expos[0] + expos[1] + expos[2], axis=0, keepdims=True)
            inverse = 1.0 / totals
            weights = jnp.concatenate([(e * inverse).astype(jnp.bfloat16) for e in expos], axis=0)
            mixed = jnp.dot(values, weights, preferred_element_type=jnp.float32)
            out_ref[:, h * HEAD_SIZE : (h + 1) * HEAD_SIZE] = mixed.T.astype(jnp.bfloat16)
            low, high = mixed[:HALF], mixed[HALF:]
            keep_ref[h * HALF : (h + 1) * HALF, :] = jnp.where(core == 0, low, high).astype(jnp.bfloat16)
            send_ref[h * HALF : (h + 1) * HALF, :] = jnp.where(core == 0, high, low).astype(jnp.bfloat16)


def attention(core, q, own, one, two, tags):
    vmem = pl.BlockSpec(memory_space=pltpu.VMEM)
    return pl.pallas_call(
        attention_kernel,
        out_shape=(
            jax.ShapeDtypeStruct((TOKENS, QUERY_HEADS * HEAD_SIZE), jnp.bfloat16),
            jax.ShapeDtypeStruct((QUERY_HEADS * HALF, TOKENS), jnp.bfloat16),
            jax.ShapeDtypeStruct((QUERY_HEADS * HALF, TOKENS), jnp.bfloat16),
        ),
        in_specs=[pl.BlockSpec(memory_space=pltpu.SMEM)] + [vmem] * 5,
        out_specs=(vmem, vmem, vmem),
        compiler_params=pltpu.CompilerParams(vmem_limit_bytes=VMEM_LIMIT),
        cost_estimate=pl.CostEstimate(
            flops=4 * QUERY_HEADS * TOKENS * 3 * TOKENS * HEAD_SIZE * 8,
            bytes_accessed=4 << 20,
            transcendentals=QUERY_HEADS * TOKENS * 3 * TOKENS,
        ),
    )(core, q, own, one, two, tags)


def outer_kernel(keep_ref, got_ref, own_ref, sib_ref, out_ref):
    total = lax.dot_general(keep_ref[...], own_ref[...], NT, preferred_element_type=jnp.float32)
    total += lax.dot_general(got_ref[...], sib_ref[...], NT, preferred_element_type=jnp.float32)
    out_ref[...] = total.astype(jnp.bfloat16)


def outer(keep, got, own, sib):
    rows, step = keep.shape[0], 256
    return pl.pallas_call(
        outer_kernel,
        out_shape=jax.ShapeDtypeStruct((rows, R), jnp.bfloat16),
        grid=(rows // step,),
        in_specs=[
            pl.BlockSpec((step, TOKENS), lambda i: (i, 0)),
            pl.BlockSpec((step, TOKENS), lambda i: (i, 0)),
            pl.BlockSpec((R, TOKENS), lambda i: (0, 0)),
            pl.BlockSpec((R, TOKENS), lambda i: (0, 0)),
        ],
        out_specs=pl.BlockSpec((step, R), lambda i: (i, 0)),
        compiler_params=pltpu.CompilerParams(vmem_limit_bytes=VMEM_LIMIT),
    )(keep, got, own, sib)


def local(queries, keys, values, doc_ids, coeffs, shard_dest, basis):
    seq = lax.axis_index("seq")
    rep = lax.axis_index("rep")
    bf16 = jnp.bfloat16

    own = jnp.concatenate([keys[0], values[0]], axis=1)
    two = shifted(own, 2)
    one = shifted(own, 1)

    gram_rows = R // REP
    basis_rows = lax.dynamic_slice_in_dim(basis, rep * gram_rows, gram_rows, 0)
    gram = lax.dot_general(basis_rows, basis, NT, preferred_element_type=jnp.float32)
    pieces = coeffs[0].T.reshape(SEQ, 4, TOKENS)
    extra = jnp.concatenate(
        [
            gram.astype(bf16).reshape(SEQ, 1, TOKENS),
            jnp.broadcast_to(shard_dest[0, 0].astype(bf16), (SEQ, 1, TOKENS)),
            jnp.broadcast_to(doc_ids[0].astype(bf16), (SEQ, 1, TOKENS)),
            jnp.zeros((SEQ, 1, TOKENS), bf16),
        ],
        axis=1,
    )
    first = lax.all_to_all(
        jnp.concatenate([pieces, extra], axis=2), "seq", split_axis=0, concat_axis=0, tiled=True
    )

    dest = first[:, 1, TOKENS].astype(jnp.int32)
    chosen = (dest[None, :] == jnp.arange(SEQ, dtype=jnp.int32)[:, None]).astype(bf16)
    sorted_own = jnp.einsum(
        "bj,jit->bit", chosen, first[:, :, :TOKENS], preferred_element_type=jnp.float32
    ).astype(bf16)
    chosen_sib = (dest[None, :] == (jnp.arange(SEQ, dtype=jnp.int32) ^ 1)[:, None]).astype(bf16)
    sorted_sib = jnp.einsum(
        "bj,jit->bit", chosen_sib, first[:, :, :TOKENS], preferred_element_type=jnp.float32
    ).astype(bf16)
    gram_piece = jnp.sum(first[:, 0, TOKENS:].astype(jnp.float32), axis=0).astype(bf16)
    second = lax.all_to_all(
        jnp.concatenate(
            [sorted_own, sorted_sib, jnp.broadcast_to(gram_piece, (SEQ, 4, TOKENS))], axis=2
        ),
        "seq",
        split_axis=0,
        concat_axis=0,
        tiled=True,
    )

    tag_rows = first[:, 2, TOKENS:].astype(jnp.float32)
    places = seq + jnp.arange(-2, 1, dtype=jnp.int32)
    tags = jnp.where(
        (places >= 0)[:, None], jnp.take(tag_rows, jnp.maximum(places, 0), axis=0), jnp.float32(-1)
    )
    core = (seq % 2).astype(jnp.int32).reshape(1)
    attended, keep, send = attention(core, queries[0], own, one, two, tags)
    got = other_core(send)

    coeffs_own = second[:, :, :TOKENS].reshape(R, TOKENS)
    coeffs_sib = second[:, :, TOKENS : 2 * TOKENS].reshape(R, TOKENS)
    partial = outer(keep, got, coeffs_own, coeffs_sib).reshape(CHIPS, HALF, R)
    arrived = lax.all_to_all(
        partial,
        "seq",
        split_axis=0,
        concat_axis=0,
        axis_index_groups=[list(range(0, SEQ, 2)), list(range(1, SEQ, 2))],
        tiled=True,
    )
    rows = jnp.sum(arrived.astype(jnp.float32), axis=0).astype(bf16)
    gram_share = second[:, 0, 2 * TOKENS :].reshape(gram_rows, R)
    last = lax.all_to_all(
        jnp.broadcast_to(jnp.concatenate([rows, gram_share], axis=0), (REP, HALF + gram_rows, R)),
        "rep",
        split_axis=0,
        concat_axis=0,
        tiled=True,
    )
    summed = jnp.sum(last[:, :HALF].astype(jnp.float32), axis=0)
    gram_all = last[:, HALF:].reshape(R, R).astype(jnp.float32)
    grad = jnp.dot(summed, gram_all, precision=lax.Precision.HIGHEST)
    grad = grad * (1.0 / math.sqrt(REP * SEQ * TOKENS))
    return attended[None], grad


def solution(mesh):
    in_specs = (
        P("rep", "seq", None),
        P("rep", "seq", None),
        P("rep", "seq", None),
        P("rep", "seq"),
        P("rep", "seq", None),
        P("rep", "seq"),
        P(None, "seq"),
    )
    out_specs = (P("rep", "seq", None), P("seq", None))
    return jax.shard_map(local, mesh=mesh, in_specs=in_specs, out_specs=out_specs, check_vma=False)
```

```python
import math

import jax
import jax.numpy as jnp
from jax import lax
from jax.experimental import pallas as pl
from jax.experimental.pallas import tpu as pltpu
from jax.sharding import PartitionSpec as P

QUERY_HEADS = 32
KEY_VALUE_HEADS = 4
HEAD_SIZE = 128
GROUP = QUERY_HEADS // KEY_VALUE_HEADS
KV = KEY_VALUE_HEADS * HEAD_SIZE
TOKENS = 128
R = 256
SEQ = 64
REP = 8
HALF = HEAD_SIZE // 2
LOG2E = math.log2(math.e)
VMEM_LIMIT = 48 * 1024 * 1024
NT = (((1,), (1,)), ((), ()))

MEMBERS = 4
SHARES = SEQ // MEMBERS
FOURS = [
    [z2 * 32 + zp * 16 + y * 2 + c for zp in range(2) for c in range(2)]
    for z2 in range(2)
    for y in range(8)
]
SIXTEENS = [list(column) for column in zip(*FOURS)]


def shifted(block, distance):
    return lax.ppermute(block, "seq", [(i, i + distance) for i in range(SEQ - distance)])


def exchange(block, axis, groups=None):
    return lax.all_to_all(
        block, axis, split_axis=0, concat_axis=0, axis_index_groups=groups, tiled=True
    )


def attention_kernel(q_ref, own_ref, one_ref, two_ref, tag_ref, out_ref, parts_ref):
    square = (TOKENS, TOKENS)
    query_tags = jnp.broadcast_to(tag_ref[...].astype(jnp.float32), square) + 1.0
    lower = lax.broadcasted_iota(jnp.int32, square, 0) <= lax.broadcasted_iota(jnp.int32, square, 1)
    tags = lambda block: block[:, 2 * KV :].astype(jnp.float32)
    wide = lambda mask: jnp.concatenate([mask] * GROUP, axis=1)
    seen_edge = wide(jnp.where(lower, tags(own_ref), tags(two_ref)) == query_tags)
    seen_one = wide(tags(one_ref) == query_tags)
    lower = wide(lower)
    hidden = jnp.float32(-1e30)
    factor = HEAD_SIZE ** (-0.5) * LOG2E
    for g in range(KEY_VALUE_HEADS):
        at = g * HEAD_SIZE
        turned = [
            b[:, KV + at : KV + at + HEAD_SIZE].astype(jnp.float32).T.astype(jnp.bfloat16)
            for b in (own_ref, one_ref, two_ref)
        ]
        q = jnp.concatenate(
            [
                q_ref[:, h * HEAD_SIZE : (h + 1) * HEAD_SIZE]
                for h in range(g * GROUP, (g + 1) * GROUP)
            ],
            axis=0,
        )
        score = lambda b: lax.dot_general(
            b[:, at : at + HEAD_SIZE], q, NT, preferred_element_type=jnp.float32
        )
        edge = jnp.where(seen_edge, jnp.where(lower, score(own_ref), score(two_ref)), hidden)
        one = jnp.where(seen_one, score(one_ref), hidden)
        highest = jnp.max(jnp.maximum(edge, one), axis=0, keepdims=True)
        edge = jnp.exp2((edge - highest) * factor)
        one = jnp.exp2((one - highest) * factor)
        inverse = 1.0 / jnp.sum(edge + one, axis=0, keepdims=True)
        edge = edge * inverse
        weights = jnp.concatenate(
            [
                jnp.where(lower, edge, 0.0).astype(jnp.bfloat16),
                (one * inverse).astype(jnp.bfloat16),
                jnp.where(lower, 0.0, edge).astype(jnp.bfloat16),
            ],
            axis=0,
        )
        mixed = jnp.dot(
            jnp.concatenate(turned, axis=1), weights, preferred_element_type=jnp.float32
        )
        for j in range(GROUP):
            h = g * GROUP + j
            head = mixed[:, j * HEAD_SIZE : (j + 1) * HEAD_SIZE]
            out_ref[:, h * HEAD_SIZE : (h + 1) * HEAD_SIZE] = head.T.astype(jnp.bfloat16)
            z, y = h // 8, h % 8
            row = ((z // 2) * 8 + y) * HALF
            parts_ref[(z % 2) * 2, row : row + HALF, :] = head[:HALF].astype(jnp.bfloat16)
            parts_ref[(z % 2) * 2 + 1, row : row + HALF, :] = head[HALF:].astype(jnp.bfloat16)


def attention(q, own, one, two, tag):
    vmem = pl.BlockSpec(memory_space=pltpu.VMEM)
    return pl.pallas_call(
        attention_kernel,
        out_shape=(
            jax.ShapeDtypeStruct((TOKENS, QUERY_HEADS * HEAD_SIZE), jnp.bfloat16),
            jax.ShapeDtypeStruct((MEMBERS, SHARES * HALF, TOKENS), jnp.bfloat16),
        ),
        in_specs=[vmem] * 5,
        out_specs=(vmem, vmem),
        compiler_params=pltpu.CompilerParams(vmem_limit_bytes=VMEM_LIMIT),
        cost_estimate=pl.CostEstimate(
            flops=4 * QUERY_HEADS * TOKENS * 3 * TOKENS * HEAD_SIZE * 6,
            bytes_accessed=4 << 20,
            transcendentals=QUERY_HEADS * TOKENS * 2 * TOKENS,
        ),
    )(q, own, one, two, tag)


def outer_kernel(parts_ref, coeffs_ref, out_ref):
    total = jnp.zeros(out_ref.shape, jnp.float32)
    for m in range(MEMBERS):
        total += lax.dot_general(
            parts_ref[m], coeffs_ref[m], NT, preferred_element_type=jnp.float32
        )
    out_ref[...] = total.astype(jnp.bfloat16)


def outer(parts, coeffs):
    rows = parts.shape[1]
    step = rows // 2
    return pl.pallas_call(
        outer_kernel,
        out_shape=jax.ShapeDtypeStruct((rows, R), jnp.bfloat16),
        grid=(rows // step,),
        in_specs=[
            pl.BlockSpec((MEMBERS, step, TOKENS), lambda i: (0, i, 0)),
            pl.BlockSpec((MEMBERS, R, TOKENS), lambda i: (0, 0, 0)),
        ],
        out_specs=pl.BlockSpec((step, R), lambda i: (i, 0)),
        compiler_params=pltpu.CompilerParams(vmem_limit_bytes=VMEM_LIMIT),
    )(parts, coeffs)


def local(queries, keys, values, doc_ids, coeffs, shard_dest, basis):
    rep = lax.axis_index("rep")
    bf16 = jnp.bfloat16

    numbers = jnp.broadcast_to((doc_ids[0] + 1).astype(bf16)[:, None], (TOKENS, TOKENS))
    own = jnp.concatenate([keys[0], values[0], numbers], axis=1)
    two = shifted(own, 2)
    one = shifted(own, 1)

    gram_rows = R // REP
    basis_rows = lax.dynamic_slice_in_dim(basis, rep * gram_rows, gram_rows, 0)
    gram = lax.dot_general(basis_rows, basis, NT, preferred_element_type=jnp.float32)
    extra = jnp.concatenate(
        [
            gram.astype(bf16).reshape(SEQ, 1, TOKENS),
            jnp.broadcast_to(shard_dest[0, 0].astype(bf16), (SEQ, 3, TOKENS)),
        ],
        axis=1,
    )
    first = exchange(jnp.concatenate([coeffs[0].T.reshape(SEQ, 4, TOKENS), extra], axis=2), "seq")

    attended, parts = attention(queries[0], own, one, two, doc_ids)
    parts, first = lax.optimization_barrier((parts, first))
    parts = exchange(parts, "seq", FOURS)

    dest = first[:, 1, TOKENS].astype(jnp.int32)
    device = lax.broadcasted_iota(jnp.int32, (SEQ, SEQ), 0)
    lowest = (device & 32) | (device & 14)
    sorted_pieces = [
        jnp.einsum(
            "bj,jit->bit",
            (dest[None, :] == lowest + (m // 2 * 16 + m % 2)).astype(bf16),
            first[:, :, :TOKENS],
            preferred_element_type=jnp.float32,
        ).astype(bf16)
        for m in range(MEMBERS)
    ]
    gram_piece = jnp.sum(first[:, 0, TOKENS:].astype(jnp.float32), axis=0).astype(bf16)
    second = exchange(
        jnp.concatenate(sorted_pieces + [jnp.broadcast_to(gram_piece, (SEQ, 4, TOKENS))], axis=2),
        "seq",
    )

    lined = jnp.stack(
        [second[:, :, m * TOKENS : (m + 1) * TOKENS].reshape(R, TOKENS) for m in range(MEMBERS)]
    )
    partial = outer(parts, lined).reshape(SHARES, HALF, R)
    arrived = exchange(partial, "seq", SIXTEENS)
    rows = jnp.sum(arrived.astype(jnp.float32), axis=0).astype(bf16)
    gram_share = second[:, 0, MEMBERS * TOKENS :].reshape(gram_rows, R)
    last = exchange(
        jnp.broadcast_to(jnp.concatenate([rows, gram_share], axis=0), (REP, HALF + gram_rows, R)),
        "rep",
    )
    summed = jnp.sum(last[:, :HALF].astype(jnp.float32), axis=0)
    gram_all = last[:, HALF:].reshape(R, R).astype(jnp.float32)
    grad = jnp.dot(summed, gram_all, precision=lax.Precision.HIGHEST)
    grad = grad * (1.0 / math.sqrt(REP * SEQ * TOKENS))
    return attended[None], grad


def solution(mesh):
    in_specs = (
        P("rep", "seq", None),
        P("rep", "seq", None),
        P("rep", "seq", None),
        P("rep", "seq"),
        P("rep", "seq", None),
        P("rep", "seq"),
        P(None, "seq"),
    )
    out_specs = (P("rep", "seq", None), P("seq", None))
    return jax.shard_map(local, mesh=mesh, in_specs=in_specs, out_specs=out_specs, check_vma=False)
```

```python
import math

import jax
import jax.numpy as jnp
from jax import lax
from jax.experimental import pallas as pl
from jax.experimental.pallas import tpu as pltpu
from jax.sharding import PartitionSpec as P

QUERY_HEADS = 32
KEY_VALUE_HEADS = 4
HEAD_SIZE = 128
GROUP = QUERY_HEADS // KEY_VALUE_HEADS
KV = KEY_VALUE_HEADS * HEAD_SIZE
TOKENS = 128
R = 256
SEQ = 64
REP = 8
HALF = HEAD_SIZE // 2
LOG2E = math.log2(math.e)
VMEM_LIMIT = 48 * 1024 * 1024
NT = (((1,), (1,)), ((), ()))

PARTNERS = (0, 1, 16, 17)
MEMBERS = len(PARTNERS)
SHARES = SEQ // MEMBERS
SIXTEENS = [
    [z2 * 32 + zp * 16 + y * 2 + c for z2 in range(2) for y in range(8)]
    for zp in range(2)
    for c in range(2)
]


def shifted(block, distance):
    return lax.ppermute(block, "seq", [(i, i + distance) for i in range(SEQ - distance)])


def swapped(block, partner):
    return lax.ppermute(block, "seq", [(i, i ^ partner) for i in range(SEQ)])


def exchange(block, axis, groups=None):
    return lax.all_to_all(
        block, axis, split_axis=0, concat_axis=0, axis_index_groups=groups, tiled=True
    )


def attention_kernel(
    place_ref, q_ref, own_ref, one_ref, two_ref, tag_ref, out_ref, *part_refs
):
    core, odd = place_ref[0], place_ref[1]
    square = (TOKENS, TOKENS)
    query_tags = jnp.broadcast_to(tag_ref[...].astype(jnp.float32), square) + 1.0
    lower = lax.broadcasted_iota(jnp.int32, square, 0) <= lax.broadcasted_iota(jnp.int32, square, 1)
    tags = lambda block: block[:, 2 * KV :].astype(jnp.float32)
    wide = lambda mask: jnp.concatenate([mask] * GROUP, axis=1)
    seen_edge = wide(jnp.where(lower, tags(own_ref), tags(two_ref)) == query_tags)
    seen_one = wide(tags(one_ref) == query_tags)
    lower = wide(lower)
    hidden = jnp.float32(-1e30)
    factor = HEAD_SIZE ** (-0.5) * LOG2E
    column = lambda start: pl.ds(pl.multiple_of(start, HEAD_SIZE), HEAD_SIZE)
    for step in range(KEY_VALUE_HEADS):
        other, z2 = step // 2, step % 2
        z = z2 * 2 + (odd if other == 0 else 1 - odd)
        at = z * HEAD_SIZE
        turned = [
            b[:, column(KV + at)].astype(jnp.float32).T.astype(jnp.bfloat16)
            for b in (own_ref, one_ref, two_ref)
        ]
        heads = [(z * GROUP + j) * HEAD_SIZE for j in range(GROUP)]
        q = jnp.concatenate([q_ref[:, column(h)] for h in heads], axis=0)
        score = lambda b: lax.dot_general(
            b[:, column(at)], q, NT, preferred_element_type=jnp.float32
        )
        edge = jnp.where(seen_edge, jnp.where(lower, score(own_ref), score(two_ref)), hidden)
        one = jnp.where(seen_one, score(one_ref), hidden)
        highest = jnp.max(jnp.maximum(edge, one), axis=0, keepdims=True)
        edge = jnp.exp2((edge - highest) * factor)
        one = jnp.exp2((one - highest) * factor)
        inverse = 1.0 / jnp.sum(edge + one, axis=0, keepdims=True)
        edge = edge * inverse
        weights = jnp.concatenate(
            [
                jnp.where(lower, edge, 0.0).astype(jnp.bfloat16),
                (one * inverse).astype(jnp.bfloat16),
                jnp.where(lower, 0.0, edge).astype(jnp.bfloat16),
            ],
            axis=0,
        )
        mixed = jnp.dot(
            jnp.concatenate(turned, axis=1), weights, preferred_element_type=jnp.float32
        )
        for j in range(GROUP):
            head = mixed[:, j * HEAD_SIZE : (j + 1) * HEAD_SIZE]
            out_ref[:, column(heads[j])] = head.T.astype(jnp.bfloat16)
            low, high = head[:HALF], head[HALF:]
            row = (z2 * 8 + j) * HALF
            part_refs[other * 2][row : row + HALF, :] = jnp.where(core == 0, low, high).astype(
                jnp.bfloat16
            )
            part_refs[other * 2 + 1][row : row + HALF, :] = jnp.where(core == 0, high, low).astype(
                jnp.bfloat16
            )


def attention(place, q, own, one, two, tag):
    vmem = pl.BlockSpec(memory_space=pltpu.VMEM)
    return pl.pallas_call(
        attention_kernel,
        out_shape=[jax.ShapeDtypeStruct((TOKENS, QUERY_HEADS * HEAD_SIZE), jnp.bfloat16)]
        + [jax.ShapeDtypeStruct((SHARES * HALF, TOKENS), jnp.bfloat16)] * MEMBERS,
        in_specs=[pl.BlockSpec(memory_space=pltpu.SMEM)] + [vmem] * 5,
        out_specs=[vmem] * (1 + MEMBERS),
        compiler_params=pltpu.CompilerParams(vmem_limit_bytes=VMEM_LIMIT),
        cost_estimate=pl.CostEstimate(
            flops=4 * QUERY_HEADS * TOKENS * 3 * TOKENS * HEAD_SIZE * 6,
            bytes_accessed=4 << 20,
            transcendentals=QUERY_HEADS * TOKENS * 2 * TOKENS,
        ),
    )(place, q, own, one, two, tag)


def outer_kernel(coeffs_ref, *refs):
    total = jnp.zeros(refs[-1].shape, jnp.float32)
    for m in range(MEMBERS):
        total += lax.dot_general(
            refs[m][...], coeffs_ref[m], NT, preferred_element_type=jnp.float32
        )
    refs[-1][...] = total.astype(jnp.bfloat16)


def outer(coeffs, parts):
    rows = parts[0].shape[0]
    step = rows // 2
    return pl.pallas_call(
        outer_kernel,
        out_shape=jax.ShapeDtypeStruct((rows, R), jnp.bfloat16),
        grid=(rows // step,),
        in_specs=[pl.BlockSpec((MEMBERS, R, TOKENS), lambda i: (0, 0, 0))]
        + [pl.BlockSpec((step, TOKENS), lambda i: (i, 0))] * MEMBERS,
        out_specs=pl.BlockSpec((step, R), lambda i: (i, 0)),
        compiler_params=pltpu.CompilerParams(vmem_limit_bytes=VMEM_LIMIT),
    )(coeffs, *parts)


def local(queries, keys, values, doc_ids, coeffs, shard_dest, basis):
    rep = lax.axis_index("rep")
    bf16 = jnp.bfloat16

    numbers = jnp.broadcast_to((doc_ids[0] + 1).astype(bf16)[:, None], (TOKENS, TOKENS))
    own = jnp.concatenate([keys[0], values[0], numbers], axis=1)
    two = shifted(own, 2)
    one = shifted(own, 1)

    gram_rows = R // REP
    basis_rows = lax.dynamic_slice_in_dim(basis, rep * gram_rows, gram_rows, 0)
    gram = lax.dot_general(basis_rows, basis, NT, preferred_element_type=jnp.float32)
    extra = jnp.concatenate(
        [
            gram.astype(bf16).reshape(SEQ, 1, TOKENS),
            jnp.broadcast_to(shard_dest[0, 0].astype(bf16), (SEQ, 3, TOKENS)),
        ],
        axis=1,
    )
    first = exchange(jnp.concatenate([coeffs[0].T.reshape(SEQ, 4, TOKENS), extra], axis=2), "seq")

    seq = lax.axis_index("seq").astype(jnp.int32)
    place = jnp.stack([seq % 2, seq // 16 % 2])
    attended, *parts = attention(place, queries[0], own, one, two, doc_ids)
    first, parts[0] = lax.optimization_barrier((first, parts[0]))
    parts = parts[:1] + [swapped(part, partner) for part, partner in zip(parts[1:], PARTNERS[1:])]

    dest = first[:, 1, TOKENS].astype(jnp.int32)
    device = lax.broadcasted_iota(jnp.int32, (SEQ, SEQ), 0)
    sorted_pieces = [
        jnp.einsum(
            "bj,jit->bit",
            (dest[None, :] == (device ^ partner)).astype(bf16),
            first[:, :, :TOKENS],
            preferred_element_type=jnp.float32,
        ).astype(bf16)
        for partner in PARTNERS
    ]
    gram_piece = jnp.sum(first[:, 0, TOKENS:].astype(jnp.float32), axis=0).astype(bf16)
    second = exchange(
        jnp.concatenate(sorted_pieces + [jnp.broadcast_to(gram_piece, (SEQ, 4, TOKENS))], axis=2),
        "seq",
    )

    lined = jnp.stack(
        [second[:, :, m * TOKENS : (m + 1) * TOKENS].reshape(R, TOKENS) for m in range(MEMBERS)]
    )
    partial = outer(lined, parts).reshape(SHARES, HALF, R)
    arrived = exchange(partial, "seq", SIXTEENS)
    rows = jnp.sum(arrived.astype(jnp.float32), axis=0).astype(bf16)
    gram_share = second[:, 0, MEMBERS * TOKENS :].reshape(gram_rows, R)
    last = exchange(
        jnp.broadcast_to(jnp.concatenate([rows, gram_share], axis=0), (REP, HALF + gram_rows, R)),
        "rep",
    )
    summed = jnp.sum(last[:, :HALF].astype(jnp.float32), axis=0)
    gram_all = last[:, HALF:].reshape(R, R).astype(jnp.float32)
    grad = jnp.dot(summed, gram_all, precision=lax.Precision.HIGHEST)
    grad = grad * (1.0 / math.sqrt(REP * SEQ * TOKENS))
    return attended[None], grad


def solution(mesh):
    in_specs = (
        P("rep", "seq", None),
        P("rep", "seq", None),
        P("rep", "seq", None),
        P("rep", "seq"),
        P("rep", "seq", None),
        P("rep", "seq"),
        P(None, "seq"),
    )
    out_specs = (P("rep", "seq", None), P("seq", None))
    return jax.shard_map(local, mesh=mesh, in_specs=in_specs, out_specs=out_specs, check_vma=False)
```

```python
import math

import jax
import jax.numpy as jnp
from jax import lax
from jax.experimental import pallas as pl
from jax.experimental.pallas import tpu as pltpu
from jax.sharding import PartitionSpec as P

QUERY_HEADS = 32
KEY_VALUE_HEADS = 4
HEAD_SIZE = 128
GROUP = QUERY_HEADS // KEY_VALUE_HEADS
KV = KEY_VALUE_HEADS * HEAD_SIZE
TOKENS = 128
R = 256
SEQ = 64
REP = 8
HALF = HEAD_SIZE // 2
LOG2E = math.log2(math.e)
VMEM_LIMIT = 48 * 1024 * 1024
PACK_VMEM_LIMIT = 66000000
NT = (((1,), (1,)), ((), ()))

PARTNERS = (0, 1, 16, 17)
MEMBERS = len(PARTNERS)
SHARES = SEQ // MEMBERS
ROWS = SHARES * HALF
SIXTEENS = [
    [z2 * 32 + zp * 16 + y * 2 + c for z2 in range(2) for y in range(8)]
    for zp in range(2)
    for c in range(2)
]


def shifted(block, distance):
    return lax.ppermute(block, "seq", [(i, i + distance) for i in range(SEQ - distance)])


def swapped(block, partner):
    return lax.ppermute(block, "seq", [(i, i ^ partner) for i in range(SEQ)])


def exchange(block, axis, groups=None):
    return lax.all_to_all(
        block, axis, split_axis=0, concat_axis=0, axis_index_groups=groups, tiled=True
    )


def attention_kernel(
    place_ref, q_ref, own_ref, one_ref, two_ref, out_ref, keep_ref, near_ref, far_ref
):
    core, odd = place_ref[0], place_ref[1]
    square = (TOKENS, TOKENS)
    lower = lax.broadcasted_iota(jnp.int32, square, 0) <= lax.broadcasted_iota(jnp.int32, square, 1)
    tags = lambda block: block[:, 2 * KV :].astype(jnp.float32)
    query_tags = tags(own_ref).T
    wide = lambda mask: jnp.concatenate([mask] * GROUP, axis=1)
    seen_edge = wide(jnp.where(lower, tags(own_ref), tags(two_ref)) == query_tags)
    seen_one = wide(tags(one_ref) == query_tags)
    lower = wide(lower)
    hidden = jnp.float32(-1e30)
    factor = HEAD_SIZE ** (-0.5) * LOG2E
    column = lambda start: pl.ds(pl.multiple_of(start, HEAD_SIZE), HEAD_SIZE)
    for step in range(KEY_VALUE_HEADS):
        other, z2 = step // 2, step % 2
        z = z2 * 2 + (odd if other == 0 else 1 - odd)
        at = z * HEAD_SIZE
        turned = [
            b[:, column(KV + at)].astype(jnp.float32).T.astype(jnp.bfloat16)
            for b in (own_ref, one_ref, two_ref)
        ]
        heads = [(z * GROUP + j) * HEAD_SIZE for j in range(GROUP)]
        q = jnp.concatenate([q_ref[:, column(h)] for h in heads], axis=0)
        score = lambda b: lax.dot_general(
            b[:, column(at)], q, NT, preferred_element_type=jnp.float32
        )
        edge = jnp.where(seen_edge, jnp.where(lower, score(own_ref), score(two_ref)), hidden)
        one = jnp.where(seen_one, score(one_ref), hidden)
        highest = jnp.max(jnp.maximum(edge, one), axis=0, keepdims=True)
        edge = jnp.exp2((edge - highest) * factor)
        one = jnp.exp2((one - highest) * factor)
        inverse = 1.0 / jnp.sum(edge + one, axis=0, keepdims=True)
        edge = edge * inverse
        weights = jnp.concatenate(
            [
                jnp.where(lower, edge, 0.0).astype(jnp.bfloat16),
                (one * inverse).astype(jnp.bfloat16),
                jnp.where(lower, 0.0, edge).astype(jnp.bfloat16),
            ],
            axis=0,
        )
        mixed = jnp.dot(
            jnp.concatenate(turned, axis=1), weights, preferred_element_type=jnp.float32
        )
        for j in range(GROUP):
            head = mixed[:, j * HEAD_SIZE : (j + 1) * HEAD_SIZE]
            out_ref[:, column(heads[j])] = head.T.astype(jnp.bfloat16)
            low, high = head[:HALF], head[HALF:]
            row = (z2 * 8 + j) * HALF
            mine = jnp.where(core == 0, low, high).astype(jnp.bfloat16)
            theirs = jnp.where(core == 0, high, low).astype(jnp.bfloat16)
            if other == 0:
                keep_ref[row : row + HALF, :] = mine
                near_ref[row : row + HALF, :] = theirs
            else:
                far_ref[row : row + HALF, :] = mine
                far_ref[ROWS + row : ROWS + row + HALF, :] = theirs


def attention(place, q, own, one, two):
    vmem = pl.BlockSpec(memory_space=pltpu.VMEM)
    return pl.pallas_call(
        attention_kernel,
        out_shape=[jax.ShapeDtypeStruct((TOKENS, QUERY_HEADS * HEAD_SIZE), jnp.bfloat16)]
        + [jax.ShapeDtypeStruct((n * ROWS, TOKENS), jnp.bfloat16) for n in (1, 1, 2)],
        in_specs=[pl.BlockSpec(memory_space=pltpu.SMEM)] + [vmem] * 4,
        out_specs=[vmem] * 4,
        compiler_params=pltpu.CompilerParams(vmem_limit_bytes=VMEM_LIMIT),
        cost_estimate=pl.CostEstimate(
            flops=4 * QUERY_HEADS * TOKENS * 3 * TOKENS * HEAD_SIZE * 6,
            bytes_accessed=4 << 20,
            transcendentals=QUERY_HEADS * TOKENS * 2 * TOKENS,
        ),
    )(place, q, own, one, two)


def outer_kernel(coeffs_ref, *refs):
    total = jnp.zeros(refs[-1].shape, jnp.float32)
    for m in range(MEMBERS):
        total += lax.dot_general(
            refs[m][...], coeffs_ref[m], NT, preferred_element_type=jnp.float32
        )
    refs[-1][...] = total.astype(jnp.bfloat16)


def outer(coeffs, keep, near, far, farthest):
    step = ROWS // 2
    block = lambda first: pl.BlockSpec((step, TOKENS), lambda i: (i + first, 0))
    return pl.pallas_call(
        outer_kernel,
        out_shape=jax.ShapeDtypeStruct((ROWS, R), jnp.bfloat16),
        grid=(ROWS // step,),
        in_specs=[
            pl.BlockSpec((MEMBERS, R, TOKENS), lambda i: (0, 0, 0)),
            block(0),
            block(0),
            block(0),
            block(ROWS // step),
        ],
        out_specs=pl.BlockSpec((step, R), lambda i: (i, 0)),
        compiler_params=pltpu.CompilerParams(vmem_limit_bytes=VMEM_LIMIT),
    )(coeffs, keep, near, far, farthest)


PIECES = (SEQ, 4, TOKENS)


def pack_kernel(
    rep_ref,
    dest_ref,
    keys_hbm,
    values_hbm,
    tag_hbm,
    coeffs_hbm,
    basis_hbm,
    own_ref,
    out_ref,
    tag_ref,
    coeffs_ref,
    basis_ref,
    sems,
):
    f32, bf16 = jnp.float32, jnp.bfloat16
    pairs = (
        (tag_hbm, tag_ref),
        (coeffs_hbm, coeffs_ref),
        (basis_hbm, basis_ref),
        (keys_hbm, own_ref.at[:, :KV]),
        (values_hbm, own_ref.at[:, KV : 2 * KV]),
    )
    copies = [pltpu.make_async_copy(a, b, sems.at[i]) for i, (a, b) in enumerate(pairs)]
    for copy in copies:
        copy.start()
    copies[0].wait()
    tags = jnp.broadcast_to(tag_ref[...].astype(f32), (TOKENS, TOKENS)).T + 1.0
    own_ref[:, 2 * KV :] = tags.astype(bf16)
    copies[1].wait()
    out_ref[:, :, :TOKENS] = coeffs_ref[...].astype(f32).T.reshape(PIECES).astype(bf16)
    copies[2].wait()
    count = R // REP
    mine = basis_ref[pl.ds(pl.multiple_of(rep_ref[0] * count, count), count), :]
    gram = lax.dot_general(mine, basis_ref[...], NT, preferred_element_type=f32)
    gram = jnp.concatenate([gram[:, :TOKENS], gram[:, TOKENS:]], axis=0).astype(bf16)
    row = lax.broadcasted_iota(jnp.int32, (R, SEQ), 0)
    column = lax.broadcasted_iota(jnp.int32, (R, SEQ), 1)
    spread = jnp.where(row == column * 4, 1.0, 0.0).astype(bf16)
    extra = jnp.dot(spread, gram, preferred_element_type=f32)
    row = lax.broadcasted_iota(jnp.int32, (R, TOKENS), 0)
    extra = jnp.where(row % 4 == 0, extra, dest_ref[0, 0].astype(f32))
    out_ref[:, :, TOKENS:] = extra.reshape(PIECES).astype(bf16)
    copies[3].wait()
    copies[4].wait()


def pack(rep, dest, keys, values, tag, coeffs, basis):
    vmem = pl.BlockSpec(memory_space=pltpu.VMEM)
    smem = pl.BlockSpec(memory_space=pltpu.SMEM)
    hbm = pl.BlockSpec(memory_space=pltpu.HBM)
    return pl.pallas_call(
        pack_kernel,
        out_shape=(
            jax.ShapeDtypeStruct((TOKENS, 2 * KV + TOKENS), jnp.bfloat16),
            jax.ShapeDtypeStruct((SEQ, 4, 2 * TOKENS), jnp.bfloat16),
        ),
        in_specs=[smem, smem] + [hbm] * 5,
        out_specs=(vmem, vmem),
        scratch_shapes=[
            pltpu.VMEM(tag.shape, tag.dtype),
            pltpu.VMEM(coeffs.shape, coeffs.dtype),
            pltpu.VMEM(basis.shape, basis.dtype),
            pltpu.SemaphoreType.DMA((5,)),
        ],
        compiler_params=pltpu.CompilerParams(vmem_limit_bytes=PACK_VMEM_LIMIT),
    )(rep, dest, keys, values, tag, coeffs, basis)


def sort_kernel(first_ref, out_ref):
    f32, bf16 = jnp.float32, jnp.bfloat16
    pieces = first_ref[:, :, :TOKENS].astype(f32).reshape(R, TOKENS).astype(bf16)
    extra = first_ref[:, :, TOKENS:].astype(f32).reshape(R, TOKENS)
    row = lax.broadcasted_iota(jnp.int32, (R, TOKENS), 0)
    gram = jnp.sum(jnp.where(row % 4 == 0, extra, 0.0), axis=0, keepdims=True)
    dest = jnp.where(row % 4 == 0, pltpu.roll(extra, R - 1, 0), extra)
    dest = jnp.concatenate([dest.T] * 2, axis=0)
    row = lax.broadcasted_iota(jnp.int32, (R, R), 0)
    column = lax.broadcasted_iota(jnp.int32, (R, R), 1)
    same = row % 4 == column % 4
    for m, partner in enumerate(PARTNERS):
        holder = ((row // 4) ^ partner).astype(f32)
        chosen = jnp.where(same & (dest == holder), 1.0, 0.0).astype(bf16)
        sorted_pieces = jnp.dot(chosen, pieces, preferred_element_type=f32)
        out_ref[:, :, m * TOKENS : (m + 1) * TOKENS] = sorted_pieces.reshape(PIECES).astype(bf16)
    out_ref[:, :, MEMBERS * TOKENS :] = jnp.broadcast_to(gram.reshape(1, 1, TOKENS), PIECES).astype(
        bf16
    )


def sort(first):
    vmem = pl.BlockSpec(memory_space=pltpu.VMEM)
    return pl.pallas_call(
        sort_kernel,
        out_shape=jax.ShapeDtypeStruct((SEQ, 4, (MEMBERS + 1) * TOKENS), jnp.bfloat16),
        in_specs=[vmem],
        out_specs=vmem,
        compiler_params=pltpu.CompilerParams(vmem_limit_bytes=VMEM_LIMIT),
    )(first)


def local(queries, keys, values, doc_ids, coeffs, shard_dest, basis):
    rep = lax.axis_index("rep").astype(jnp.int32)
    seq = lax.axis_index("seq").astype(jnp.int32)
    bf16 = jnp.bfloat16

    own, packed = pack(rep[None], shard_dest, keys[0], values[0], doc_ids, coeffs[0], basis)
    two = shifted(own, 2)
    one = shifted(own, 1)
    first = exchange(packed, "seq")

    place = jnp.stack([seq & 1, (seq >> 4) & 1])
    attended, keep, near, far = attention(place, queries[0], own, one, two)
    first, keep = lax.optimization_barrier((first, keep))
    near = swapped(near, 1)
    far = swapped(far, 16)
    farthest = swapped(far, 1)

    second = exchange(sort(first), "seq")

    lined = jnp.stack(
        [second[:, :, m * TOKENS : (m + 1) * TOKENS].reshape(R, TOKENS) for m in range(MEMBERS)]
    )
    partial = outer(lined, keep, near, far, farthest).reshape(SHARES, HALF, R)
    arrived = exchange(partial, "seq", SIXTEENS)
    rows = jnp.sum(arrived.astype(jnp.float32), axis=0).astype(bf16)
    gram_rows = R // REP
    gram_share = second[:, 0, MEMBERS * TOKENS :]
    gram_share = jnp.concatenate([gram_share[:gram_rows], gram_share[gram_rows:]], axis=1)
    last = exchange(
        jnp.broadcast_to(jnp.concatenate([rows, gram_share], axis=0), (REP, HALF + gram_rows, R)),
        "rep",
    )
    summed = jnp.sum(last[:, :HALF].astype(jnp.float32), axis=0)
    gram_all = last[:, HALF:].reshape(R, R).astype(jnp.float32)
    grad = jnp.dot(summed, gram_all, precision=lax.Precision.HIGHEST)
    grad = grad * (1.0 / math.sqrt(REP * SEQ * TOKENS))
    return attended[None], grad


def solution(mesh):
    in_specs = (
        P("rep", "seq", None),
        P("rep", "seq", None),
        P("rep", "seq", None),
        P("rep", "seq"),
        P("rep", "seq", None),
        P("rep", "seq"),
        P(None, "seq"),
    )
    out_specs = (P("rep", "seq", None), P("seq", None))
    return jax.shard_map(local, mesh=mesh, in_specs=in_specs, out_specs=out_specs, check_vma=False)
```

```python
import functools
import math

import jax
import jax.numpy as jnp
from jax import lax
from jax.experimental import pallas as pl
from jax.experimental.pallas import tpu as pltpu
from jax.sharding import PartitionSpec as P

QUERY_HEADS = 32
KEY_VALUE_HEADS = 4
HEAD_SIZE = 128
GROUP = QUERY_HEADS // KEY_VALUE_HEADS
KV = KEY_VALUE_HEADS * HEAD_SIZE
TOKENS = 128
R = 256
SEQ = 64
REP = 8
HALF = HEAD_SIZE // 2
LOG2E = math.log2(math.e)
VMEM_LIMIT = 48 * 1024 * 1024
OWN_COPIES_VMEM_LIMIT = 66000000
NT = (((1,), (1,)), ((), ()))

PARTNERS = (0, 1, 16, 17)
MEMBERS = len(PARTNERS)
SHARES = SEQ // MEMBERS
ROWS = SHARES * HALF
SIXTEENS = [
    [z2 * 32 + zp * 16 + y * 2 + c for z2 in range(2) for y in range(8)]
    for zp in range(2)
    for c in range(2)
]


def shifted(block, distance):
    return lax.ppermute(block, "seq", [(i, i + distance) for i in range(SEQ - distance)])


def swapped(block, partner):
    return lax.ppermute(block, "seq", [(i, i ^ partner) for i in range(SEQ)])


def exchange(block, axis, groups=None):
    return lax.all_to_all(
        block, axis, split_axis=0, concat_axis=0, axis_index_groups=groups, tiled=True
    )


def attention_kernel(other, place_ref, q_hbm, own_hbm, one_hbm, two_hbm, *refs):
    if other == 0:
        _, out_hbm, mine_ref, theirs_ref = refs[:4]
    else:
        out_hbm, mine_ref = refs[:2]
        theirs_ref = mine_ref
    q_ref, block_ref, tag_ref, out_ref, sems = refs[-5:]
    core, odd = place_ref[0], place_ref[1]
    blocks = (own_hbm, one_hbm, two_hbm)
    span = GROUP * HEAD_SIZE
    columns = lambda start, size: pl.ds(pl.multiple_of(start, size), size)
    zs = [z2 * 2 + (odd if other == 0 else 1 - odd) for z2 in range(2)]
    tag_copies = [
        pltpu.make_async_copy(b.at[:, 2 * KV :], tag_ref.at[i], sems.at[i])
        for i, b in enumerate(blocks)
    ]
    steps = []
    for z2, z in enumerate(zs):
        at = 3 + z2 * 7
        copies = [
            pltpu.make_async_copy(q_hbm.at[:, columns(z * span, span)], q_ref.at[z2], sems.at[at])
        ]
        for i, b in enumerate(blocks):
            for part in range(2):
                copies.append(
                    pltpu.make_async_copy(
                        b.at[:, columns(part * KV + z * HEAD_SIZE, HEAD_SIZE)],
                        block_ref.at[z2, part, i],
                        sems.at[at + 1 + i * 2 + part],
                    )
                )
        steps.append(copies)
    for copy in tag_copies + steps[0] + steps[1]:
        copy.start()
    outs = [
        pltpu.make_async_copy(
            out_ref.at[z2], out_hbm.at[:, columns(z * span, span)], sems.at[17 + z2]
        )
        for z2, z in enumerate(zs)
    ]
    square = (TOKENS, TOKENS)
    lower = lax.broadcasted_iota(jnp.int32, square, 0) <= lax.broadcasted_iota(jnp.int32, square, 1)
    for copy in tag_copies:
        copy.wait()
    own_tags, one_tags, two_tags = [tag_ref[i].astype(jnp.float32) for i in range(3)]
    query_tags = own_tags.T
    wide = lambda mask: jnp.concatenate([mask] * GROUP, axis=1)
    seen_edge = wide(jnp.where(lower, own_tags, two_tags) == query_tags)
    seen_one = wide(one_tags == query_tags)
    lower = wide(lower)
    hidden = jnp.float32(-1e30)
    factor = HEAD_SIZE ** (-0.5) * LOG2E
    for z2 in range(2):
        for copy in steps[z2]:
            copy.wait()
        turned = [block_ref[z2, 1, i].astype(jnp.float32).T.astype(jnp.bfloat16) for i in range(3)]
        q = jnp.concatenate(
            [q_ref[z2, :, j * HEAD_SIZE : (j + 1) * HEAD_SIZE] for j in range(GROUP)], axis=0
        )
        score = lambda i: lax.dot_general(
            block_ref[z2, 0, i], q, NT, preferred_element_type=jnp.float32
        )
        edge = jnp.where(seen_edge, jnp.where(lower, score(0), score(2)), hidden)
        one = jnp.where(seen_one, score(1), hidden)
        highest = jnp.max(jnp.maximum(edge, one), axis=0, keepdims=True)
        edge = jnp.exp2((edge - highest) * factor)
        one = jnp.exp2((one - highest) * factor)
        inverse = 1.0 / jnp.sum(edge + one, axis=0, keepdims=True)
        edge = edge * inverse
        weights = jnp.concatenate(
            [
                jnp.where(lower, edge, 0.0).astype(jnp.bfloat16),
                (one * inverse).astype(jnp.bfloat16),
                jnp.where(lower, 0.0, edge).astype(jnp.bfloat16),
            ],
            axis=0,
        )
        mixed = jnp.dot(
            jnp.concatenate(turned, axis=1), weights, preferred_element_type=jnp.float32
        )
        for j in range(GROUP):
            head = mixed[:, j * HEAD_SIZE : (j + 1) * HEAD_SIZE]
            out_ref[z2, :, j * HEAD_SIZE : (j + 1) * HEAD_SIZE] = head.T.astype(jnp.bfloat16)
            low, high = head[:HALF], head[HALF:]
            row = (z2 * 8 + j) * HALF
            shift = other * ROWS
            mine_ref[row : row + HALF, :] = jnp.where(core == 0, low, high).astype(jnp.bfloat16)
            theirs_ref[shift + row : shift + row + HALF, :] = jnp.where(
                core == 0, high, low
            ).astype(jnp.bfloat16)
        outs[z2].start()
    for copy in outs:
        copy.wait()


def attention(other, place, q, own, one, two, attended=None):
    vmem = pl.BlockSpec(memory_space=pltpu.VMEM)
    hbm = pl.BlockSpec(memory_space=pltpu.HBM)
    operands = (place, q, own, one, two) + (() if attended is None else (attended,))
    sizes = (2,) if other else (1, 1)
    square = (TOKENS, TOKENS)
    return pl.pallas_call(
        functools.partial(attention_kernel, other),
        out_shape=[jax.ShapeDtypeStruct((TOKENS, QUERY_HEADS * HEAD_SIZE), jnp.bfloat16)]
        + [jax.ShapeDtypeStruct((n * ROWS, TOKENS), jnp.bfloat16) for n in sizes],
        in_specs=[pl.BlockSpec(memory_space=pltpu.SMEM)] + [hbm] * (len(operands) - 1),
        out_specs=[hbm] + [vmem] * len(sizes),
        scratch_shapes=[
            pltpu.VMEM((2, TOKENS, GROUP * HEAD_SIZE), jnp.bfloat16),
            pltpu.VMEM((2, 2, 3) + square, jnp.bfloat16),
            pltpu.VMEM((3,) + square, jnp.bfloat16),
            pltpu.VMEM((2, TOKENS, GROUP * HEAD_SIZE), jnp.bfloat16),
            pltpu.SemaphoreType.DMA((19,)),
        ],
        input_output_aliases={} if attended is None else {5: 0},
        compiler_params=pltpu.CompilerParams(vmem_limit_bytes=OWN_COPIES_VMEM_LIMIT),
        cost_estimate=pl.CostEstimate(
            flops=4 * QUERY_HEADS * TOKENS * 3 * TOKENS * HEAD_SIZE * 3,
            bytes_accessed=2 << 20,
            transcendentals=QUERY_HEADS * TOKENS * TOKENS,
        ),
    )(*operands)


def outer_kernel(coeffs_ref, *refs):
    total = jnp.zeros(refs[-1].shape, jnp.float32)
    for m in range(MEMBERS):
        total += lax.dot_general(
            refs[m][...], coeffs_ref[m], NT, preferred_element_type=jnp.float32
        )
    refs[-1][...] = total.astype(jnp.bfloat16)


def outer(coeffs, keep, near, far, farthest):
    step = ROWS // 2
    block = lambda first: pl.BlockSpec((step, TOKENS), lambda i: (i + first, 0))
    return pl.pallas_call(
        outer_kernel,
        out_shape=jax.ShapeDtypeStruct((ROWS, R), jnp.bfloat16),
        grid=(ROWS // step,),
        in_specs=[
            pl.BlockSpec((MEMBERS, R, TOKENS), lambda i: (0, 0, 0)),
            block(0),
            block(0),
            block(0),
            block(ROWS // step),
        ],
        out_specs=pl.BlockSpec((step, R), lambda i: (i, 0)),
        compiler_params=pltpu.CompilerParams(vmem_limit_bytes=VMEM_LIMIT),
    )(coeffs, keep, near, far, farthest)


PIECES = (SEQ, 4, TOKENS)


def pack_kernel(
    rep_ref,
    dest_ref,
    keys_hbm,
    values_hbm,
    tag_hbm,
    coeffs_hbm,
    basis_hbm,
    own_ref,
    out_ref,
    tag_ref,
    coeffs_ref,
    basis_ref,
    sems,
):
    f32, bf16 = jnp.float32, jnp.bfloat16
    pairs = (
        (tag_hbm, tag_ref),
        (coeffs_hbm, coeffs_ref),
        (basis_hbm, basis_ref),
        (keys_hbm, own_ref.at[:, :KV]),
        (values_hbm, own_ref.at[:, KV : 2 * KV]),
    )
    copies = [pltpu.make_async_copy(a, b, sems.at[i]) for i, (a, b) in enumerate(pairs)]
    for copy in copies:
        copy.start()
    copies[0].wait()
    tags = jnp.broadcast_to(tag_ref[...].astype(f32), (TOKENS, TOKENS)).T + 1.0
    own_ref[:, 2 * KV :] = tags.astype(bf16)
    copies[1].wait()
    out_ref[:, :, :TOKENS] = coeffs_ref[...].astype(f32).T.reshape(PIECES).astype(bf16)
    copies[2].wait()
    count = R // REP
    mine = basis_ref[pl.ds(pl.multiple_of(rep_ref[0] * count, count), count), :]
    gram = lax.dot_general(mine, basis_ref[...], NT, preferred_element_type=f32)
    gram = jnp.concatenate([gram[:, :TOKENS], gram[:, TOKENS:]], axis=0).astype(bf16)
    row = lax.broadcasted_iota(jnp.int32, (R, SEQ), 0)
    column = lax.broadcasted_iota(jnp.int32, (R, SEQ), 1)
    spread = jnp.where(row == column * 4, 1.0, 0.0).astype(bf16)
    extra = jnp.dot(spread, gram, preferred_element_type=f32)
    row = lax.broadcasted_iota(jnp.int32, (R, TOKENS), 0)
    extra = jnp.where(row % 4 == 0, extra, dest_ref[0, 0].astype(f32))
    out_ref[:, :, TOKENS:] = extra.reshape(PIECES).astype(bf16)
    copies[3].wait()
    copies[4].wait()


def pack(rep, dest, keys, values, tag, coeffs, basis):
    vmem = pl.BlockSpec(memory_space=pltpu.VMEM)
    smem = pl.BlockSpec(memory_space=pltpu.SMEM)
    hbm = pl.BlockSpec(memory_space=pltpu.HBM)
    return pl.pallas_call(
        pack_kernel,
        out_shape=(
            jax.ShapeDtypeStruct((TOKENS, 2 * KV + TOKENS), jnp.bfloat16),
            jax.ShapeDtypeStruct((SEQ, 4, 2 * TOKENS), jnp.bfloat16),
        ),
        in_specs=[smem, smem] + [hbm] * 5,
        out_specs=(vmem, vmem),
        scratch_shapes=[
            pltpu.VMEM(tag.shape, tag.dtype),
            pltpu.VMEM(coeffs.shape, coeffs.dtype),
            pltpu.VMEM(basis.shape, basis.dtype),
            pltpu.SemaphoreType.DMA((5,)),
        ],
        compiler_params=pltpu.CompilerParams(vmem_limit_bytes=OWN_COPIES_VMEM_LIMIT),
    )(rep, dest, keys, values, tag, coeffs, basis)


def sort_kernel(first_ref, out_ref):
    f32, bf16 = jnp.float32, jnp.bfloat16
    pieces = first_ref[:, :, :TOKENS].astype(f32).reshape(R, TOKENS).astype(bf16)
    extra = first_ref[:, :, TOKENS:].astype(f32).reshape(R, TOKENS)
    row = lax.broadcasted_iota(jnp.int32, (R, TOKENS), 0)
    gram = jnp.sum(jnp.where(row % 4 == 0, extra, 0.0), axis=0, keepdims=True)
    dest = jnp.where(row % 4 == 0, pltpu.roll(extra, R - 1, 0), extra)
    dest = jnp.concatenate([dest.T] * 2, axis=0)
    row = lax.broadcasted_iota(jnp.int32, (R, R), 0)
    column = lax.broadcasted_iota(jnp.int32, (R, R), 1)
    same = row % 4 == column % 4
    for m, partner in enumerate(PARTNERS):
        holder = ((row // 4) ^ partner).astype(f32)
        chosen = jnp.where(same & (dest == holder), 1.0, 0.0).astype(bf16)
        sorted_pieces = jnp.dot(chosen, pieces, preferred_element_type=f32)
        out_ref[:, :, m * TOKENS : (m + 1) * TOKENS] = sorted_pieces.reshape(PIECES).astype(bf16)
    out_ref[:, :, MEMBERS * TOKENS :] = jnp.broadcast_to(gram.reshape(1, 1, TOKENS), PIECES).astype(
        bf16
    )


def sort(first):
    vmem = pl.BlockSpec(memory_space=pltpu.VMEM)
    return pl.pallas_call(
        sort_kernel,
        out_shape=jax.ShapeDtypeStruct((SEQ, 4, (MEMBERS + 1) * TOKENS), jnp.bfloat16),
        in_specs=[vmem],
        out_specs=vmem,
        compiler_params=pltpu.CompilerParams(vmem_limit_bytes=VMEM_LIMIT),
    )(first)


def local(queries, keys, values, doc_ids, coeffs, shard_dest, basis):
    rep = lax.axis_index("rep").astype(jnp.int32)
    seq = lax.axis_index("seq").astype(jnp.int32)
    bf16 = jnp.bfloat16

    own, packed = pack(rep[None], shard_dest, keys[0], values[0], doc_ids, coeffs[0], basis)
    two = shifted(own, 2)
    one = shifted(own, 1)
    first = exchange(packed, "seq")

    place = jnp.stack([seq & 1, (seq >> 4) & 1])
    attended, far = attention(1, place, queries[0], own, one, two)
    first, far = lax.optimization_barrier((first, far))
    far = swapped(far, 16)

    second = exchange(sort(first), "seq")
    attended, keep, near = attention(0, place, queries[0], own, one, two, attended)
    near, far = lax.optimization_barrier((near, far))
    near = swapped(near, 1)
    farthest = swapped(far, 1)

    lined = jnp.stack(
        [second[:, :, m * TOKENS : (m + 1) * TOKENS].reshape(R, TOKENS) for m in range(MEMBERS)]
    )
    partial = outer(lined, keep, near, far, farthest).reshape(SHARES, HALF, R)
    arrived = exchange(partial, "seq", SIXTEENS)
    rows = jnp.sum(arrived.astype(jnp.float32), axis=0).astype(bf16)
    gram_rows = R // REP
    gram_share = second[:, 0, MEMBERS * TOKENS :]
    gram_share = jnp.concatenate([gram_share[:gram_rows], gram_share[gram_rows:]], axis=1)
    last = exchange(
        jnp.broadcast_to(jnp.concatenate([rows, gram_share], axis=0), (REP, HALF + gram_rows, R)),
        "rep",
    )
    summed = jnp.sum(last[:, :HALF].astype(jnp.float32), axis=0)
    gram_all = last[:, HALF:].reshape(R, R).astype(jnp.float32)
    grad = jnp.dot(summed, gram_all, precision=lax.Precision.HIGHEST)
    grad = grad * (1.0 / math.sqrt(REP * SEQ * TOKENS))
    return attended[None], grad


def solution(mesh):
    in_specs = (
        P("rep", "seq", None),
        P("rep", "seq", None),
        P("rep", "seq", None),
        P("rep", "seq"),
        P("rep", "seq", None),
        P("rep", "seq"),
        P(None, "seq"),
    )
    out_specs = (P("rep", "seq", None), P("seq", None))
    return jax.shard_map(local, mesh=mesh, in_specs=in_specs, out_specs=out_specs, check_vma=False)
```

```python
import functools
import math

import jax
import jax.numpy as jnp
from jax import lax
from jax.experimental import pallas as pl
from jax.experimental.pallas import tpu as pltpu
from jax.sharding import PartitionSpec as P

QUERY_HEADS = 32
KEY_VALUE_HEADS = 4
HEAD_SIZE = 128
GROUP = QUERY_HEADS // KEY_VALUE_HEADS
KV = KEY_VALUE_HEADS * HEAD_SIZE
TOKENS = 128
R = 256
SEQ = 64
REP = 8
HALF = HEAD_SIZE // 2
LOG2E = math.log2(math.e)
VMEM_LIMIT = 48 * 1024 * 1024
PACK_VMEM_LIMIT = 66000000
NT = (((1,), (1,)), ((), ()))

PARTNERS = (0, 1, 16, 17)
MEMBERS = len(PARTNERS)
SHARES = SEQ // MEMBERS
ROWS = SHARES * HALF
SIXTEENS = [
    [z2 * 32 + zp * 16 + y * 2 + c for z2 in range(2) for y in range(8)]
    for zp in range(2)
    for c in range(2)
]


def shifted(block, distance):
    return lax.ppermute(block, "seq", [(i, i + distance) for i in range(SEQ - distance)])


def swapped(block, partner):
    return lax.ppermute(block, "seq", [(i, i ^ partner) for i in range(SEQ)])


def exchange(block, axis, groups=None):
    return lax.all_to_all(
        block, axis, split_axis=0, concat_axis=0, axis_index_groups=groups, tiled=True
    )


def attention_kernel(other, q_ref, own_ref, one_ref, two_ref, *refs):
    if other == 0:
        half_ref, out_ref, mine_ref, theirs_ref = refs
    else:
        half_ref, mine_ref = refs
        theirs_ref = mine_ref
    seq = lax.axis_index("seq")
    core, odd = seq & 1, (seq >> 4) & 1
    square = (TOKENS, TOKENS)
    lower = lax.broadcasted_iota(jnp.int32, square, 0) <= lax.broadcasted_iota(jnp.int32, square, 1)
    tags = lambda block: block[:, 2 * KV :].astype(jnp.float32)
    query_tags = tags(own_ref).T
    wide = lambda mask: jnp.concatenate([mask] * GROUP, axis=1)
    seen_edge = wide(jnp.where(lower, tags(own_ref), tags(two_ref)) == query_tags)
    seen_one = wide(tags(one_ref) == query_tags)
    lower = wide(lower)
    hidden = jnp.float32(-1e30)
    factor = HEAD_SIZE ** (-0.5) * LOG2E
    column = lambda start: pl.ds(pl.multiple_of(start, HEAD_SIZE), HEAD_SIZE)
    span = GROUP * HEAD_SIZE
    for z2 in range(2):
        z = z2 * 2 + (odd if other == 0 else 1 - odd)
        at = z * HEAD_SIZE
        turned = [
            b[:, column(KV + at)].astype(jnp.float32).T.astype(jnp.bfloat16)
            for b in (own_ref, one_ref, two_ref)
        ]
        heads = [(z * GROUP + j) * HEAD_SIZE for j in range(GROUP)]
        q = jnp.concatenate([q_ref[:, column(h)] for h in heads], axis=0)
        score = lambda b: lax.dot_general(
            b[:, column(at)], q, NT, preferred_element_type=jnp.float32
        )
        edge = jnp.where(seen_edge, jnp.where(lower, score(own_ref), score(two_ref)), hidden)
        one = jnp.where(seen_one, score(one_ref), hidden)
        highest = jnp.max(jnp.maximum(edge, one), axis=0, keepdims=True)
        edge = jnp.exp2((edge - highest) * factor)
        one = jnp.exp2((one - highest) * factor)
        inverse = 1.0 / jnp.sum(edge + one, axis=0, keepdims=True)
        edge = edge * inverse
        weights = jnp.concatenate(
            [
                jnp.where(lower, edge, 0.0).astype(jnp.bfloat16),
                (one * inverse).astype(jnp.bfloat16),
                jnp.where(lower, 0.0, edge).astype(jnp.bfloat16),
            ],
            axis=0,
        )
        mixed = jnp.dot(
            jnp.concatenate(turned, axis=1), weights, preferred_element_type=jnp.float32
        )
        for j in range(GROUP):
            head = mixed[:, j * HEAD_SIZE : (j + 1) * HEAD_SIZE]
            turned = head.T.astype(jnp.bfloat16)
            if other == 0:
                out_ref[:, column(heads[j])] = turned
            else:
                at = z2 * span + j * HEAD_SIZE
                half_ref[:, at : at + HEAD_SIZE] = turned
            low, high = head[:HALF], head[HALF:]
            row = (z2 * 8 + j) * HALF
            shift = other * ROWS
            mine_ref[row : row + HALF, :] = jnp.where(core == 0, low, high).astype(jnp.bfloat16)
            theirs_ref[shift + row : shift + row + HALF, :] = jnp.where(
                core == 0, high, low
            ).astype(jnp.bfloat16)
        if other == 0:
            away = pl.ds(pl.multiple_of((z2 * 2 + 1 - odd) * span, span), span)
            out_ref[:, away] = half_ref[:, z2 * span : (z2 + 1) * span]


def attention(other, q, own, one, two, *half):
    vmem = pl.BlockSpec(memory_space=pltpu.VMEM)
    width = QUERY_HEADS * HEAD_SIZE
    shapes = [(TOKENS, width // 2), (2 * ROWS, TOKENS)]
    if other == 0:
        shapes = [(TOKENS, width), (ROWS, TOKENS), (ROWS, TOKENS)]
    return pl.pallas_call(
        functools.partial(attention_kernel, other),
        out_shape=[jax.ShapeDtypeStruct(shape, jnp.bfloat16) for shape in shapes],
        in_specs=[vmem] * (4 + len(half)),
        out_specs=[vmem] * len(shapes),
        compiler_params=pltpu.CompilerParams(vmem_limit_bytes=VMEM_LIMIT),
        cost_estimate=pl.CostEstimate(
            flops=1 << 20, bytes_accessed=1 << 18, transcendentals=1 << 10
        )
        if other
        else pl.CostEstimate(flops=3 << 30, bytes_accessed=2 << 20, transcendentals=1 << 19),
    )(q, own, one, two, *half)


def outer_kernel(coeffs_ref, *refs):
    total = jnp.zeros(refs[-1].shape, jnp.float32)
    for m in range(MEMBERS):
        total += lax.dot_general(
            refs[m][...], coeffs_ref[m], NT, preferred_element_type=jnp.float32
        )
    refs[-1][...] = total.astype(jnp.bfloat16)


def outer(coeffs, keep, near, far, farthest):
    step = ROWS // 2
    block = lambda first: pl.BlockSpec((step, TOKENS), lambda i: (i + first, 0))
    return pl.pallas_call(
        outer_kernel,
        out_shape=jax.ShapeDtypeStruct((ROWS, R), jnp.bfloat16),
        grid=(ROWS // step,),
        in_specs=[
            pl.BlockSpec((MEMBERS, R, TOKENS), lambda i: (0, 0, 0)),
            block(0),
            block(0),
            block(0),
            block(ROWS // step),
        ],
        out_specs=pl.BlockSpec((step, R), lambda i: (i, 0)),
        compiler_params=pltpu.CompilerParams(vmem_limit_bytes=VMEM_LIMIT),
    )(coeffs, keep, near, far, farthest)


PIECES = (SEQ, 4, TOKENS)


def pack_kernel(
    dest_hbm,
    keys_hbm,
    values_hbm,
    tag_hbm,
    coeffs_hbm,
    basis_hbm,
    own_ref,
    out_ref,
    dest_ref,
    tag_ref,
    coeffs_ref,
    basis_ref,
    sems,
):
    f32, bf16 = jnp.float32, jnp.bfloat16
    pairs = (
        (tag_hbm, tag_ref),
        (coeffs_hbm, coeffs_ref),
        (basis_hbm, basis_ref),
        (keys_hbm, own_ref.at[:, :KV]),
        (values_hbm, own_ref.at[:, KV : 2 * KV]),
        (dest_hbm, dest_ref),
    )
    copies = [pltpu.make_async_copy(a, b, sems.at[i]) for i, (a, b) in enumerate(pairs)]
    for copy in copies:
        copy.start()
    copies[0].wait()
    tags = jnp.broadcast_to(tag_ref[...].astype(f32), (TOKENS, TOKENS)).T + 1.0
    own_ref[:, 2 * KV :] = tags.astype(bf16)
    copies[1].wait()
    out_ref[:, :, :TOKENS] = coeffs_ref[...].astype(f32).T.reshape(PIECES).astype(bf16)
    copies[2].wait()
    count = R // REP
    mine = basis_ref[pl.ds(pl.multiple_of(lax.axis_index("rep") * count, count), count), :]
    gram = lax.dot_general(mine, basis_ref[...], NT, preferred_element_type=f32)
    gram = jnp.concatenate([gram[:, :TOKENS], gram[:, TOKENS:]], axis=0).astype(bf16)
    row = lax.broadcasted_iota(jnp.int32, (R, SEQ), 0)
    column = lax.broadcasted_iota(jnp.int32, (R, SEQ), 1)
    spread = jnp.where(row == column * 4, 1.0, 0.0).astype(bf16)
    extra = jnp.dot(spread, gram, preferred_element_type=f32)
    row = lax.broadcasted_iota(jnp.int32, (R, TOKENS), 0)
    copies[5].wait()
    extra = jnp.where(row % 4 == 0, extra, dest_ref[0, 0].astype(f32))
    out_ref[:, :, TOKENS:] = extra.reshape(PIECES).astype(bf16)
    copies[3].wait()
    copies[4].wait()


def pack(dest, keys, values, tag, coeffs, basis):
    vmem = pl.BlockSpec(memory_space=pltpu.VMEM)
    hbm = pl.BlockSpec(memory_space=pltpu.HBM)
    return pl.pallas_call(
        pack_kernel,
        out_shape=(
            jax.ShapeDtypeStruct((TOKENS, 2 * KV + TOKENS), jnp.bfloat16),
            jax.ShapeDtypeStruct((SEQ, 4, 2 * TOKENS), jnp.bfloat16),
        ),
        in_specs=[hbm] * 6,
        out_specs=(vmem, vmem),
        scratch_shapes=[
            pltpu.SMEM(dest.shape, dest.dtype),
            pltpu.VMEM(tag.shape, tag.dtype),
            pltpu.VMEM(coeffs.shape, coeffs.dtype),
            pltpu.VMEM(basis.shape, basis.dtype),
            pltpu.SemaphoreType.DMA((6,)),
        ],
        compiler_params=pltpu.CompilerParams(vmem_limit_bytes=PACK_VMEM_LIMIT),
    )(dest, keys, values, tag, coeffs, basis)


def sort_kernel(first_ref, out_ref):
    f32, bf16 = jnp.float32, jnp.bfloat16
    pieces = first_ref[:, :, :TOKENS].astype(f32).reshape(R, TOKENS).astype(bf16)
    extra = first_ref[:, :, TOKENS:].astype(f32).reshape(R, TOKENS)
    row = lax.broadcasted_iota(jnp.int32, (R, TOKENS), 0)
    gram = jnp.sum(jnp.where(row % 4 == 0, extra, 0.0), axis=0, keepdims=True)
    dest = jnp.where(row % 4 == 0, pltpu.roll(extra, R - 1, 0), extra)
    dest = jnp.concatenate([dest.T] * 2, axis=0)
    row = lax.broadcasted_iota(jnp.int32, (R, R), 0)
    column = lax.broadcasted_iota(jnp.int32, (R, R), 1)
    same = row % 4 == column % 4
    for m, partner in enumerate(PARTNERS):
        holder = ((row // 4) ^ partner).astype(f32)
        chosen = jnp.where(same & (dest == holder), 1.0, 0.0).astype(bf16)
        sorted_pieces = jnp.dot(chosen, pieces, preferred_element_type=f32)
        out_ref[:, :, m * TOKENS : (m + 1) * TOKENS] = sorted_pieces.reshape(PIECES).astype(bf16)
    out_ref[:, :, MEMBERS * TOKENS :] = jnp.broadcast_to(gram.reshape(1, 1, TOKENS), PIECES).astype(
        bf16
    )


def sort(first):
    vmem = pl.BlockSpec(memory_space=pltpu.VMEM)
    return pl.pallas_call(
        sort_kernel,
        out_shape=jax.ShapeDtypeStruct((SEQ, 4, (MEMBERS + 1) * TOKENS), jnp.bfloat16),
        in_specs=[vmem],
        out_specs=vmem,
        compiler_params=pltpu.CompilerParams(vmem_limit_bytes=VMEM_LIMIT),
    )(first)


def local(queries, keys, values, doc_ids, coeffs, shard_dest, basis):
    bf16 = jnp.bfloat16

    own, packed = pack(shard_dest, keys[0], values[0], doc_ids, coeffs[0], basis)
    two = shifted(own, 2)
    one = shifted(own, 1)
    first = exchange(packed, "seq")

    half, far = attention(1, queries[0], own, one, two)
    first, half = lax.optimization_barrier((first, half))
    far = swapped(far, 16)

    second = exchange(sort(first), "seq")
    attended, keep, near = attention(0, queries[0], own, one, two, half)
    near, far = lax.optimization_barrier((near, far))
    near = swapped(near, 1)
    farthest = swapped(far, 1)

    lined = jnp.stack(
        [second[:, :, m * TOKENS : (m + 1) * TOKENS].reshape(R, TOKENS) for m in range(MEMBERS)]
    )
    partial = outer(lined, keep, near, far, farthest).reshape(SHARES, HALF, R)
    arrived = exchange(partial, "seq", SIXTEENS)
    rows = jnp.sum(arrived.astype(jnp.float32), axis=0).astype(bf16)
    gram_rows = R // REP
    gram_share = second[:, 0, MEMBERS * TOKENS :]
    gram_share = jnp.concatenate([gram_share[:gram_rows], gram_share[gram_rows:]], axis=1)
    last = exchange(
        jnp.broadcast_to(jnp.concatenate([rows, gram_share], axis=0), (REP, HALF + gram_rows, R)),
        "rep",
    )
    summed = jnp.sum(last[:, :HALF].astype(jnp.float32), axis=0)
    gram_all = last[:, HALF:].reshape(R, R).astype(jnp.float32)
    grad = jnp.dot(summed, gram_all, precision=lax.Precision.HIGHEST)
    grad = grad * (1.0 / math.sqrt(REP * SEQ * TOKENS))
    return attended[None], grad


def solution(mesh):
    in_specs = (
        P("rep", "seq", None),
        P("rep", "seq", None),
        P("rep", "seq", None),
        P("rep", "seq"),
        P("rep", "seq", None),
        P("rep", "seq"),
        P(None, "seq"),
    )
    out_specs = (P("rep", "seq", None), P("seq", None))
    return jax.shard_map(local, mesh=mesh, in_specs=in_specs, out_specs=out_specs, check_vma=False)
```

```python
import functools
import math

import jax
import jax.numpy as jnp
from jax import lax
from jax.experimental import pallas as pl
from jax.experimental.pallas import tpu as pltpu
from jax.sharding import PartitionSpec as P

QUERY_HEADS = 32
KEY_VALUE_HEADS = 4
HEAD_SIZE = 128
GROUP = QUERY_HEADS // KEY_VALUE_HEADS
KV = KEY_VALUE_HEADS * HEAD_SIZE
TOKENS = 128
R = 256
SEQ = 64
REP = 8
HALF = HEAD_SIZE // 2
LOG2E = math.log2(math.e)
VMEM_LIMIT = 48 * 1024 * 1024
PACK_VMEM_LIMIT = 66000000
NT = (((1,), (1,)), ((), ()))

PARTNERS = (0, 1, 16, 17)
MEMBERS = len(PARTNERS)
SHARES = SEQ // MEMBERS
ROWS = SHARES * HALF
SIXTEENS = [
    [z2 * 32 + zp * 16 + y * 2 + c for z2 in range(2) for y in range(8)]
    for zp in range(2)
    for c in range(2)
]


def shifted(block, distance):
    return lax.ppermute(block, "seq", [(i, i + distance) for i in range(SEQ - distance)])


def swapped(block, partner):
    return lax.ppermute(block, "seq", [(i, i ^ partner) for i in range(SEQ)])


def exchange(block, axis, groups=None):
    return lax.all_to_all(
        block, axis, split_axis=0, concat_axis=0, axis_index_groups=groups, tiled=True
    )


def attention_kernel(other, q_ref, own_ref, one_ref, two_ref, *refs):
    if other == 0:
        half_ref, out_ref, mine_ref, theirs_ref = refs
    else:
        half_ref, mine_ref = refs
        theirs_ref = mine_ref
    seq = lax.axis_index("seq")
    core, odd = seq & 1, (seq >> 4) & 1
    square = (TOKENS, TOKENS)
    lower = lax.broadcasted_iota(jnp.int32, square, 0) <= lax.broadcasted_iota(jnp.int32, square, 1)
    tags = lambda block: block[:, 2 * KV :].astype(jnp.float32)
    query_tags = tags(own_ref).T
    wide = lambda mask: jnp.concatenate([mask] * GROUP, axis=1)
    seen_edge = wide(jnp.where(lower, tags(own_ref), tags(two_ref)) == query_tags)
    seen_one = wide(tags(one_ref) == query_tags)
    lower = wide(lower)
    hidden = jnp.float32(-1e30)
    factor = HEAD_SIZE ** (-0.5) * LOG2E
    column = lambda start: pl.ds(pl.multiple_of(start, HEAD_SIZE), HEAD_SIZE)
    span = GROUP * HEAD_SIZE
    for z2 in range(2):
        z = z2 * 2 + (odd if other == 0 else 1 - odd)
        at = z * HEAD_SIZE
        turned = [
            b[:, column(KV + at)].astype(jnp.float32).T.astype(jnp.bfloat16)
            for b in (own_ref, one_ref, two_ref)
        ]
        heads = [(z * GROUP + j) * HEAD_SIZE for j in range(GROUP)]
        q = jnp.concatenate([q_ref[:, column(h)] for h in heads], axis=0)
        score = lambda b: lax.dot_general(
            b[:, column(at)], q, NT, preferred_element_type=jnp.float32
        )
        edge = jnp.where(seen_edge, jnp.where(lower, score(own_ref), score(two_ref)), hidden)
        one = jnp.where(seen_one, score(one_ref), hidden)
        highest = jnp.max(jnp.maximum(edge, one), axis=0, keepdims=True)
        edge = jnp.exp2((edge - highest) * factor)
        one = jnp.exp2((one - highest) * factor)
        inverse = 1.0 / jnp.sum(edge + one, axis=0, keepdims=True)
        edge = edge * inverse
        weights = jnp.concatenate(
            [
                jnp.where(lower, edge, 0.0).astype(jnp.bfloat16),
                (one * inverse).astype(jnp.bfloat16),
                jnp.where(lower, 0.0, edge).astype(jnp.bfloat16),
            ],
            axis=0,
        )
        mixed = jnp.dot(
            jnp.concatenate(turned, axis=1), weights, preferred_element_type=jnp.float32
        )
        for j in range(GROUP):
            head = mixed[:, j * HEAD_SIZE : (j + 1) * HEAD_SIZE]
            turned = head.T.astype(jnp.bfloat16)
            if other == 0:
                out_ref[:, column(heads[j])] = turned
            else:
                at = z2 * span + j * HEAD_SIZE
                half_ref[:, at : at + HEAD_SIZE] = turned
            low, high = head[:HALF], head[HALF:]
            row = (z2 * 8 + j) * HALF
            shift = other * ROWS
            mine_ref[row : row + HALF, :] = jnp.where(core == 0, low, high).astype(jnp.bfloat16)
            theirs_ref[shift + row : shift + row + HALF, :] = jnp.where(
                core == 0, high, low
            ).astype(jnp.bfloat16)
        if other == 0:
            away = pl.ds(pl.multiple_of((z2 * 2 + 1 - odd) * span, span), span)
            out_ref[:, away] = half_ref[:, z2 * span : (z2 + 1) * span]


def attention(other, q, own, one, two, *half):
    vmem = pl.BlockSpec(memory_space=pltpu.VMEM)
    width = QUERY_HEADS * HEAD_SIZE
    shapes = [(TOKENS, width // 2), (2 * ROWS, TOKENS)]
    if other == 0:
        shapes = [(TOKENS, width), (ROWS, TOKENS), (ROWS, TOKENS)]
    return pl.pallas_call(
        functools.partial(attention_kernel, other),
        out_shape=[jax.ShapeDtypeStruct(shape, jnp.bfloat16) for shape in shapes],
        in_specs=[vmem] * (4 + len(half)),
        out_specs=[vmem] * len(shapes),
        compiler_params=pltpu.CompilerParams(vmem_limit_bytes=VMEM_LIMIT),
        cost_estimate=pl.CostEstimate(
            flops=1 << 20, bytes_accessed=1 << 18, transcendentals=1 << 10
        )
        if other
        else pl.CostEstimate(flops=3 << 30, bytes_accessed=2 << 20, transcendentals=1 << 19),
    )(q, own, one, two, *half)


def outer_kernel(second_ref, keep_ref, near_ref, far_ref, farthest_ref, out_ref, coeffs_ref):
    pair = 2 * TOKENS

    @pl.when(pl.program_id(0) == 0)
    def _():
        for p in range(MEMBERS // 2):
            part = second_ref[:, :, p * pair : (p + 1) * pair].astype(jnp.float32)
            coeffs_ref[p] = part.reshape(R, pair).astype(jnp.bfloat16)

    total = jnp.zeros(out_ref.shape, jnp.float32)
    for p, refs in enumerate(((keep_ref, near_ref), (far_ref, farthest_ref))):
        total += lax.dot_general(
            jnp.concatenate([ref[...] for ref in refs], axis=1),
            coeffs_ref[p],
            NT,
            preferred_element_type=jnp.float32,
        )
    out_ref[...] = total.astype(jnp.bfloat16)


def outer(second, keep, near, far, farthest):
    step = ROWS // 2
    block = lambda first: pl.BlockSpec((step, TOKENS), lambda i: (i + first, 0))
    return pl.pallas_call(
        outer_kernel,
        out_shape=jax.ShapeDtypeStruct((ROWS, R), jnp.bfloat16),
        grid=(ROWS // step,),
        in_specs=[
            pl.BlockSpec(second.shape, lambda i: (0, 0, 0)),
            block(0),
            block(0),
            block(0),
            block(ROWS // step),
        ],
        out_specs=pl.BlockSpec((step, R), lambda i: (i, 0)),
        scratch_shapes=[pltpu.VMEM((MEMBERS // 2, R, 2 * TOKENS), jnp.bfloat16)],
        compiler_params=pltpu.CompilerParams(vmem_limit_bytes=VMEM_LIMIT),
    )(second, keep, near, far, farthest)


PIECES = (SEQ, 4, TOKENS)


def pack_kernel(
    dest_hbm,
    keys_hbm,
    values_hbm,
    tag_hbm,
    coeffs_hbm,
    basis_hbm,
    own_ref,
    out_ref,
    dest_ref,
    tag_ref,
    coeffs_ref,
    basis_ref,
    sems,
):
    f32, bf16 = jnp.float32, jnp.bfloat16
    pairs = (
        (tag_hbm, tag_ref),
        (coeffs_hbm, coeffs_ref),
        (basis_hbm, basis_ref),
        (keys_hbm, own_ref.at[:, :KV]),
        (values_hbm, own_ref.at[:, KV : 2 * KV]),
        (dest_hbm, dest_ref),
    )
    copies = [pltpu.make_async_copy(a, b, sems.at[i]) for i, (a, b) in enumerate(pairs)]
    for copy in copies:
        copy.start()
    copies[0].wait()
    tags = jnp.broadcast_to(tag_ref[...].astype(f32), (TOKENS, TOKENS)).T + 1.0
    own_ref[:, 2 * KV :] = tags.astype(bf16)
    copies[1].wait()
    out_ref[:, :, :TOKENS] = coeffs_ref[...].astype(f32).T.reshape(PIECES).astype(bf16)
    copies[2].wait()
    count = R // REP
    mine = basis_ref[pl.ds(pl.multiple_of(lax.axis_index("rep") * count, count), count), :]
    gram = lax.dot_general(mine, basis_ref[...], NT, preferred_element_type=f32)
    gram = jnp.concatenate([gram[:, :TOKENS], gram[:, TOKENS:]], axis=0).astype(bf16)
    row = lax.broadcasted_iota(jnp.int32, (R, SEQ), 0)
    column = lax.broadcasted_iota(jnp.int32, (R, SEQ), 1)
    spread = jnp.where(row == column * 4, 1.0, 0.0).astype(bf16)
    extra = jnp.dot(spread, gram, preferred_element_type=f32)
    row = lax.broadcasted_iota(jnp.int32, (R, TOKENS), 0)
    copies[5].wait()
    extra = jnp.where(row % 4 == 0, extra, dest_ref[0, 0].astype(f32))
    out_ref[:, :, TOKENS:] = extra.reshape(PIECES).astype(bf16)
    copies[3].wait()
    copies[4].wait()


def pack(dest, keys, values, tag, coeffs, basis):
    vmem = pl.BlockSpec(memory_space=pltpu.VMEM)
    hbm = pl.BlockSpec(memory_space=pltpu.HBM)
    return pl.pallas_call(
        pack_kernel,
        out_shape=(
            jax.ShapeDtypeStruct((TOKENS, 2 * KV + TOKENS), jnp.bfloat16),
            jax.ShapeDtypeStruct((SEQ, 4, 2 * TOKENS), jnp.bfloat16),
        ),
        in_specs=[hbm] * 6,
        out_specs=(vmem, vmem),
        scratch_shapes=[
            pltpu.SMEM(dest.shape, dest.dtype),
            pltpu.VMEM(tag.shape, tag.dtype),
            pltpu.VMEM(coeffs.shape, coeffs.dtype),
            pltpu.VMEM(basis.shape, basis.dtype),
            pltpu.SemaphoreType.DMA((6,)),
        ],
        compiler_params=pltpu.CompilerParams(vmem_limit_bytes=PACK_VMEM_LIMIT),
    )(dest, keys, values, tag, coeffs, basis)


def sort_kernel(first_ref, out_ref):
    f32, bf16 = jnp.float32, jnp.bfloat16
    pieces = first_ref[:, :, :TOKENS].astype(f32).reshape(R, TOKENS).astype(bf16)
    extra = first_ref[:, :, TOKENS:].astype(f32).reshape(R, TOKENS)
    row = lax.broadcasted_iota(jnp.int32, (R, TOKENS), 0)
    gram = jnp.sum(jnp.where(row % 4 == 0, extra, 0.0), axis=0, keepdims=True)
    dest = jnp.where(row % 4 == 0, pltpu.roll(extra, R - 1, 0), extra)
    dest = jnp.concatenate([dest.T] * 2, axis=0)
    row = lax.broadcasted_iota(jnp.int32, (R, R), 0)
    column = lax.broadcasted_iota(jnp.int32, (R, R), 1)
    same = row % 4 == column % 4
    for m, partner in enumerate(PARTNERS):
        holder = ((row // 4) ^ partner).astype(f32)
        chosen = jnp.where(same & (dest == holder), 1.0, 0.0).astype(bf16)
        sorted_pieces = jnp.dot(chosen, pieces, preferred_element_type=f32)
        out_ref[:, :, m * TOKENS : (m + 1) * TOKENS] = sorted_pieces.reshape(PIECES).astype(bf16)
    out_ref[:, :, MEMBERS * TOKENS :] = jnp.broadcast_to(gram.reshape(1, 1, TOKENS), PIECES).astype(
        bf16
    )


def sort(first):
    vmem = pl.BlockSpec(memory_space=pltpu.VMEM)
    return pl.pallas_call(
        sort_kernel,
        out_shape=jax.ShapeDtypeStruct((SEQ, 4, (MEMBERS + 1) * TOKENS), jnp.bfloat16),
        in_specs=[vmem],
        out_specs=vmem,
        compiler_params=pltpu.CompilerParams(vmem_limit_bytes=VMEM_LIMIT),
    )(first)


def local(queries, keys, values, doc_ids, coeffs, shard_dest, basis):
    bf16 = jnp.bfloat16

    own, packed = pack(shard_dest, keys[0], values[0], doc_ids, coeffs[0], basis)
    two = shifted(own, 2)
    one = shifted(own, 1)
    first = exchange(packed, "seq")

    half, far = attention(1, queries[0], own, one, two)
    first, half = lax.optimization_barrier((first, half))
    far = swapped(far, 16)

    second = exchange(sort(first), "seq")
    attended, keep, near = attention(0, queries[0], own, one, two, half)
    near, far = lax.optimization_barrier((near, far))
    near = swapped(near, 1)
    farthest = swapped(far, 1)

    partial = outer(second, keep, near, far, farthest).reshape(SHARES, HALF, R)
    arrived = exchange(partial, "seq", SIXTEENS)
    rows = jnp.sum(arrived.astype(jnp.float32), axis=0).astype(bf16)
    gram_rows = R // REP
    gram_share = second[:, 0, MEMBERS * TOKENS :]
    gram_share = jnp.concatenate([gram_share[:gram_rows], gram_share[gram_rows:]], axis=1)
    last = exchange(
        jnp.broadcast_to(jnp.concatenate([rows, gram_share], axis=0), (REP, HALF + gram_rows, R)),
        "rep",
    )
    summed = jnp.sum(last[:, :HALF].astype(jnp.float32), axis=0)
    gram_all = last[:, HALF:].reshape(R, R).astype(jnp.float32)
    grad = jnp.dot(summed, gram_all, precision=lax.Precision.HIGHEST)
    grad = grad * (1.0 / math.sqrt(REP * SEQ * TOKENS))
    return attended[None], grad


def solution(mesh):
    in_specs = (
        P("rep", "seq", None),
        P("rep", "seq", None),
        P("rep", "seq", None),
        P("rep", "seq"),
        P("rep", "seq", None),
        P("rep", "seq"),
        P(None, "seq"),
    )
    out_specs = (P("rep", "seq", None), P("seq", None))
    return jax.shard_map(local, mesh=mesh, in_specs=in_specs, out_specs=out_specs, check_vma=False)
```

```python
import functools
import math

import jax
import jax.numpy as jnp
from jax import lax
from jax.experimental import pallas as pl
from jax.experimental.pallas import tpu as pltpu
from jax.sharding import PartitionSpec as P

QUERY_HEADS = 32
KEY_VALUE_HEADS = 4
HEAD_SIZE = 128
GROUP = QUERY_HEADS // KEY_VALUE_HEADS
KV = KEY_VALUE_HEADS * HEAD_SIZE
TOKENS = 128
R = 256
SEQ = 64
REP = 8
HALF = HEAD_SIZE // 2
LOG2E = math.log2(math.e)
VMEM_LIMIT = 48 * 1024 * 1024
PACK_VMEM_LIMIT = 66000000
NT = (((1,), (1,)), ((), ()))

PARTNERS = (0, 1, 16, 17)
MEMBERS = len(PARTNERS)
SHARES = SEQ // MEMBERS
ROWS = SHARES * HALF
SIXTEENS = [
    [z2 * 32 + zp * 16 + y * 2 + c for z2 in range(2) for y in range(8)]
    for zp in range(2)
    for c in range(2)
]


def shifted(block, distance):
    return lax.ppermute(block, "seq", [(i, i + distance) for i in range(SEQ - distance)])


def swapped(block, partner):
    return lax.ppermute(block, "seq", [(i, i ^ partner) for i in range(SEQ)])


def exchange(block, axis, groups=None):
    return lax.all_to_all(
        block, axis, split_axis=0, concat_axis=0, axis_index_groups=groups, tiled=True
    )


def attention_kernel(other, q_ref, own_ref, one_ref, two_ref, *refs):
    slab_ref, sems = refs[-2:]
    if other == 0:
        _, out_hbm, mine_ref, theirs_ref = refs[:-2]
    else:
        out_hbm, mine_ref, mark_ref = refs[:-2]
        theirs_ref = mine_ref
        mark_ref[...] = jnp.zeros(mark_ref.shape, mark_ref.dtype)
    leaving = []
    seq = lax.axis_index("seq")
    core, odd = seq & 1, (seq >> 4) & 1
    square = (TOKENS, TOKENS)
    lower = lax.broadcasted_iota(jnp.int32, square, 0) <= lax.broadcasted_iota(jnp.int32, square, 1)
    tags = lambda block: block[:, 2 * KV :].astype(jnp.float32)
    query_tags = tags(own_ref).T
    wide = lambda mask: jnp.concatenate([mask] * GROUP, axis=1)
    seen_edge = wide(jnp.where(lower, tags(own_ref), tags(two_ref)) == query_tags)
    seen_one = wide(tags(one_ref) == query_tags)
    lower = wide(lower)
    hidden = jnp.float32(-1e30)
    factor = HEAD_SIZE ** (-0.5) * LOG2E
    column = lambda start: pl.ds(pl.multiple_of(start, HEAD_SIZE), HEAD_SIZE)
    span = GROUP * HEAD_SIZE
    for z2 in range(2):
        z = z2 * 2 + (odd if other == 0 else 1 - odd)
        at = z * HEAD_SIZE
        turned = [
            b[:, column(KV + at)].astype(jnp.float32).T.astype(jnp.bfloat16)
            for b in (own_ref, one_ref, two_ref)
        ]
        heads = [(z * GROUP + j) * HEAD_SIZE for j in range(GROUP)]
        q = jnp.concatenate([q_ref[:, column(h)] for h in heads], axis=0)
        score = lambda b: lax.dot_general(
            b[:, column(at)], q, NT, preferred_element_type=jnp.float32
        )
        edge = jnp.where(seen_edge, jnp.where(lower, score(own_ref), score(two_ref)), hidden)
        one = jnp.where(seen_one, score(one_ref), hidden)
        highest = jnp.max(jnp.maximum(edge, one), axis=0, keepdims=True)
        edge = jnp.exp2((edge - highest) * factor)
        one = jnp.exp2((one - highest) * factor)
        inverse = 1.0 / jnp.sum(edge + one, axis=0, keepdims=True)
        edge = edge * inverse
        weights = jnp.concatenate(
            [
                jnp.where(lower, edge, 0.0).astype(jnp.bfloat16),
                (one * inverse).astype(jnp.bfloat16),
                jnp.where(lower, 0.0, edge).astype(jnp.bfloat16),
            ],
            axis=0,
        )
        mixed = jnp.dot(
            jnp.concatenate(turned, axis=1), weights, preferred_element_type=jnp.float32
        )
        for j in range(GROUP):
            head = mixed[:, j * HEAD_SIZE : (j + 1) * HEAD_SIZE]
            slab_ref[z2, :, j * HEAD_SIZE : (j + 1) * HEAD_SIZE] = head.T.astype(jnp.bfloat16)
            low, high = head[:HALF], head[HALF:]
            row = (z2 * 8 + j) * HALF
            shift = other * ROWS
            mine_ref[row : row + HALF, :] = jnp.where(core == 0, low, high).astype(jnp.bfloat16)
            theirs_ref[shift + row : shift + row + HALF, :] = jnp.where(
                core == 0, high, low
            ).astype(jnp.bfloat16)
        slab = pl.ds(pl.multiple_of(z * span, span), span)
        leaving.append(pltpu.make_async_copy(slab_ref.at[z2], out_hbm.at[:, slab], sems.at[z2]))
        leaving[z2].start()
    for copy in leaving:
        copy.wait()


def attention(other, q, own, one, two, *attended):
    vmem = pl.BlockSpec(memory_space=pltpu.VMEM)
    hbm = pl.BlockSpec(memory_space=pltpu.HBM)
    shapes = [(2 * ROWS, TOKENS), (16, TOKENS)] if other else [(ROWS, TOKENS), (ROWS, TOKENS)]
    shapes = [(TOKENS, QUERY_HEADS * HEAD_SIZE)] + shapes
    return pl.pallas_call(
        functools.partial(attention_kernel, other),
        out_shape=[jax.ShapeDtypeStruct(shape, jnp.bfloat16) for shape in shapes],
        in_specs=[vmem] * 4 + [hbm] * len(attended),
        out_specs=[hbm, vmem, vmem],
        scratch_shapes=[
            pltpu.VMEM((2, TOKENS, GROUP * HEAD_SIZE), jnp.bfloat16),
            pltpu.SemaphoreType.DMA((2,)),
        ],
        input_output_aliases={4: 0} if attended else {},
        compiler_params=pltpu.CompilerParams(vmem_limit_bytes=VMEM_LIMIT),
        cost_estimate=pl.CostEstimate(
            flops=1 << 20, bytes_accessed=1 << 18, transcendentals=1 << 10
        )
        if other
        else pl.CostEstimate(flops=3 << 30, bytes_accessed=2 << 20, transcendentals=1 << 19),
    )(q, own, one, two, *attended)


def outer_kernel(second_ref, keep_ref, near_ref, far_ref, farthest_ref, out_ref, coeffs_ref):
    pair = 2 * TOKENS

    @pl.when(pl.program_id(0) == 0)
    def _():
        for p in range(MEMBERS // 2):
            part = second_ref[:, :, p * pair : (p + 1) * pair].astype(jnp.float32)
            coeffs_ref[p] = part.reshape(R, pair).astype(jnp.bfloat16)

    total = jnp.zeros(out_ref.shape, jnp.float32)
    for p, refs in enumerate(((keep_ref, near_ref), (far_ref, farthest_ref))):
        total += lax.dot_general(
            jnp.concatenate([ref[...] for ref in refs], axis=1),
            coeffs_ref[p],
            NT,
            preferred_element_type=jnp.float32,
        )
    out_ref[...] = total.astype(jnp.bfloat16)


def outer(second, keep, near, far, farthest):
    step = ROWS // 2
    block = lambda first: pl.BlockSpec((step, TOKENS), lambda i: (i + first, 0))
    return pl.pallas_call(
        outer_kernel,
        out_shape=jax.ShapeDtypeStruct((ROWS, R), jnp.bfloat16),
        grid=(ROWS // step,),
        in_specs=[
            pl.BlockSpec(second.shape, lambda i: (0, 0, 0)),
            block(0),
            block(0),
            block(0),
            block(ROWS // step),
        ],
        out_specs=pl.BlockSpec((step, R), lambda i: (i, 0)),
        scratch_shapes=[pltpu.VMEM((MEMBERS // 2, R, 2 * TOKENS), jnp.bfloat16)],
        compiler_params=pltpu.CompilerParams(vmem_limit_bytes=VMEM_LIMIT),
    )(second, keep, near, far, farthest)


PIECES = (SEQ, 4, TOKENS)


def pack_kernel(
    dest_hbm,
    keys_hbm,
    values_hbm,
    tag_hbm,
    coeffs_hbm,
    basis_hbm,
    own_ref,
    out_ref,
    dest_ref,
    tag_ref,
    coeffs_ref,
    basis_ref,
    sems,
):
    f32, bf16 = jnp.float32, jnp.bfloat16
    pairs = (
        (tag_hbm, tag_ref),
        (coeffs_hbm, coeffs_ref),
        (basis_hbm, basis_ref),
        (keys_hbm, own_ref.at[:, :KV]),
        (values_hbm, own_ref.at[:, KV : 2 * KV]),
        (dest_hbm, dest_ref),
    )
    copies = [pltpu.make_async_copy(a, b, sems.at[i]) for i, (a, b) in enumerate(pairs)]
    for copy in copies:
        copy.start()
    copies[0].wait()
    tags = jnp.broadcast_to(tag_ref[...].astype(f32), (TOKENS, TOKENS)).T + 1.0
    own_ref[:, 2 * KV :] = tags.astype(bf16)
    copies[1].wait()
    out_ref[:, :, :TOKENS] = coeffs_ref[...].astype(f32).T.reshape(PIECES).astype(bf16)
    copies[2].wait()
    count = R // REP
    mine = basis_ref[pl.ds(pl.multiple_of(lax.axis_index("rep") * count, count), count), :]
    gram = lax.dot_general(mine, basis_ref[...], NT, preferred_element_type=f32)
    gram = jnp.concatenate([gram[:, :TOKENS], gram[:, TOKENS:]], axis=0).astype(bf16)
    row = lax.broadcasted_iota(jnp.int32, (R, SEQ), 0)
    column = lax.broadcasted_iota(jnp.int32, (R, SEQ), 1)
    spread = jnp.where(row == column * 4, 1.0, 0.0).astype(bf16)
    extra = jnp.dot(spread, gram, preferred_element_type=f32)
    row = lax.broadcasted_iota(jnp.int32, (R, TOKENS), 0)
    copies[5].wait()
    extra = jnp.where(row % 4 == 0, extra, dest_ref[0, 0].astype(f32))
    out_ref[:, :, TOKENS:] = extra.reshape(PIECES).astype(bf16)
    copies[3].wait()
    copies[4].wait()


def pack(dest, keys, values, tag, coeffs, basis):
    vmem = pl.BlockSpec(memory_space=pltpu.VMEM)
    hbm = pl.BlockSpec(memory_space=pltpu.HBM)
    return pl.pallas_call(
        pack_kernel,
        out_shape=(
            jax.ShapeDtypeStruct((TOKENS, 2 * KV + TOKENS), jnp.bfloat16),
            jax.ShapeDtypeStruct((SEQ, 4, 2 * TOKENS), jnp.bfloat16),
        ),
        in_specs=[hbm] * 6,
        out_specs=(vmem, vmem),
        scratch_shapes=[
            pltpu.SMEM(dest.shape, dest.dtype),
            pltpu.VMEM(tag.shape, tag.dtype),
            pltpu.VMEM(coeffs.shape, coeffs.dtype),
            pltpu.VMEM(basis.shape, basis.dtype),
            pltpu.SemaphoreType.DMA((6,)),
        ],
        compiler_params=pltpu.CompilerParams(vmem_limit_bytes=PACK_VMEM_LIMIT),
    )(dest, keys, values, tag, coeffs, basis)


def sort_kernel(first_ref, mark_ref, out_ref):
    f32, bf16 = jnp.float32, jnp.bfloat16
    pieces = first_ref[:, :, :TOKENS].astype(f32).reshape(R, TOKENS).astype(bf16)
    extra = first_ref[:, :, TOKENS:].astype(f32).reshape(R, TOKENS)
    row = lax.broadcasted_iota(jnp.int32, (R, TOKENS), 0)
    gram = jnp.sum(jnp.where(row % 4 == 0, extra, 0.0), axis=0, keepdims=True)
    dest = jnp.where(row % 4 == 0, pltpu.roll(extra, R - 1, 0), extra)
    dest = jnp.concatenate([dest.T] * 2, axis=0)
    row = lax.broadcasted_iota(jnp.int32, (R, R), 0)
    column = lax.broadcasted_iota(jnp.int32, (R, R), 1)
    same = row % 4 == column % 4
    for m, partner in enumerate(PARTNERS):
        holder = ((row // 4) ^ partner).astype(f32)
        chosen = jnp.where(same & (dest == holder), 1.0, 0.0).astype(bf16)
        sorted_pieces = jnp.dot(chosen, pieces, preferred_element_type=f32)
        out_ref[:, :, m * TOKENS : (m + 1) * TOKENS] = sorted_pieces.reshape(PIECES).astype(bf16)
    out_ref[:, :, MEMBERS * TOKENS :] = jnp.broadcast_to(gram.reshape(1, 1, TOKENS), PIECES).astype(
        bf16
    )


def sort(first, mark):
    vmem = pl.BlockSpec(memory_space=pltpu.VMEM)
    return pl.pallas_call(
        sort_kernel,
        out_shape=jax.ShapeDtypeStruct((SEQ, 4, (MEMBERS + 1) * TOKENS), jnp.bfloat16),
        in_specs=[vmem, vmem],
        out_specs=vmem,
        compiler_params=pltpu.CompilerParams(vmem_limit_bytes=VMEM_LIMIT),
    )(first, mark)


def local(queries, keys, values, doc_ids, coeffs, shard_dest, basis):
    bf16 = jnp.bfloat16

    own, packed = pack(shard_dest, keys[0], values[0], doc_ids, coeffs[0], basis)
    two = shifted(own, 2)
    one = shifted(own, 1)
    first = exchange(packed, "seq")

    attended, far, mark = attention(1, queries[0], own, one, two)
    far = swapped(far, 16)

    second = exchange(sort(first, mark), "seq")
    attended, keep, near = attention(0, queries[0], own, one, two, attended)
    near, far = lax.optimization_barrier((near, far))
    near = swapped(near, 1)
    farthest = swapped(far, 1)

    partial = outer(second, keep, near, far, farthest).reshape(SHARES, HALF, R)
    arrived = exchange(partial, "seq", SIXTEENS)
    rows = jnp.sum(arrived.astype(jnp.float32), axis=0).astype(bf16)
    gram_rows = R // REP
    gram_share = second[:, 0, MEMBERS * TOKENS :]
    gram_share = jnp.concatenate([gram_share[:gram_rows], gram_share[gram_rows:]], axis=1)
    last = exchange(
        jnp.broadcast_to(jnp.concatenate([rows, gram_share], axis=0), (REP, HALF + gram_rows, R)),
        "rep",
    )
    summed = jnp.sum(last[:, :HALF].astype(jnp.float32), axis=0)
    gram_all = last[:, HALF:].reshape(R, R).astype(jnp.float32)
    grad = jnp.dot(summed, gram_all, precision=lax.Precision.HIGHEST)
    grad = grad * (1.0 / math.sqrt(REP * SEQ * TOKENS))
    return attended[None], grad


def solution(mesh):
    in_specs = (
        P("rep", "seq", None),
        P("rep", "seq", None),
        P("rep", "seq", None),
        P("rep", "seq"),
        P("rep", "seq", None),
        P("rep", "seq"),
        P(None, "seq"),
    )
    out_specs = (P("rep", "seq", None), P("seq", None))
    return jax.shard_map(local, mesh=mesh, in_specs=in_specs, out_specs=out_specs, check_vma=False)
```

```python
import functools
import math

import jax
import jax.numpy as jnp
from jax import lax
from jax.experimental import pallas as pl
from jax.experimental.pallas import tpu as pltpu
from jax.sharding import PartitionSpec as P

QUERY_HEADS = 32
KEY_VALUE_HEADS = 4
HEAD_SIZE = 128
GROUP = QUERY_HEADS // KEY_VALUE_HEADS
KV = KEY_VALUE_HEADS * HEAD_SIZE
TOKENS = 128
R = 256
SEQ = 64
REP = 8
HALF = HEAD_SIZE // 2
LOG2E = math.log2(math.e)
VMEM_LIMIT = 48 * 1024 * 1024
PACK_VMEM_LIMIT = 66000000
NT = (((1,), (1,)), ((), ()))

PARTNERS = (0, 1, 16, 17)
MEMBERS = len(PARTNERS)
SHARES = SEQ // MEMBERS
ROWS = SHARES * HALF
SIXTEENS = [
    [z2 * 32 + zp * 16 + y * 2 + c for z2 in range(2) for y in range(8)]
    for zp in range(2)
    for c in range(2)
]


def shifted(block, distance):
    return lax.ppermute(block, "seq", [(i, i + distance) for i in range(SEQ - distance)])


def swapped(block, partner):
    return lax.ppermute(block, "seq", [(i, i ^ partner) for i in range(SEQ)])


def exchange(block, axis, groups=None):
    return lax.all_to_all(
        block, axis, split_axis=0, concat_axis=0, axis_index_groups=groups, tiled=True
    )


def attention_kernel(other, q_ref, own_ref, one_ref, two_ref, *refs):
    if other == 0:
        away_ref, out_hbm, mine_ref, theirs_ref, slab_ref, sems = refs
    else:
        mine_ref, mark_ref = refs
        theirs_ref = mine_ref
        mark_ref[...] = jnp.zeros(mark_ref.shape, mark_ref.dtype)
    leaving = []
    seq = lax.axis_index("seq")
    core, odd = seq & 1, (seq >> 4) & 1
    span = GROUP * HEAD_SIZE

    def leave(z, at):
        slab = pl.ds(pl.multiple_of(z * span, span), span)
        leaving.append(pltpu.make_async_copy(slab_ref.at[at], out_hbm.at[:, slab], sems.at[at]))
        leaving[-1].start()

    if other == 0:
        for z2 in range(2):
            for j in range(GROUP):
                row = (z2 * 8 + j) * HALF
                mine = away_ref[row : row + HALF, :].astype(jnp.float32)
                theirs = away_ref[ROWS + row : ROWS + row + HALF, :].astype(jnp.float32)
                head = jnp.concatenate(
                    [jnp.where(core == 0, mine, theirs), jnp.where(core == 0, theirs, mine)], axis=0
                )
                slab_ref[2 + z2, :, j * HEAD_SIZE : (j + 1) * HEAD_SIZE] = head.T.astype(
                    jnp.bfloat16
                )
            leave(z2 * 2 + 1 - odd, 2 + z2)
    square = (TOKENS, TOKENS)
    lower = lax.broadcasted_iota(jnp.int32, square, 0) <= lax.broadcasted_iota(jnp.int32, square, 1)
    tags = lambda block: block[:, 2 * KV :].astype(jnp.float32)
    query_tags = tags(own_ref).T
    wide = lambda mask: jnp.concatenate([mask] * GROUP, axis=1)
    seen_edge = wide(jnp.where(lower, tags(own_ref), tags(two_ref)) == query_tags)
    seen_one = wide(tags(one_ref) == query_tags)
    lower = wide(lower)
    hidden = jnp.float32(-1e30)
    factor = HEAD_SIZE ** (-0.5) * LOG2E
    column = lambda start: pl.ds(pl.multiple_of(start, HEAD_SIZE), HEAD_SIZE)
    for z2 in range(2):
        z = z2 * 2 + (odd if other == 0 else 1 - odd)
        at = z * HEAD_SIZE
        turned = [
            b[:, column(KV + at)].astype(jnp.float32).T.astype(jnp.bfloat16)
            for b in (own_ref, one_ref, two_ref)
        ]
        heads = [(z * GROUP + j) * HEAD_SIZE for j in range(GROUP)]
        q = jnp.concatenate([q_ref[:, column(h)] for h in heads], axis=0)
        score = lambda b: lax.dot_general(
            b[:, column(at)], q, NT, preferred_element_type=jnp.float32
        )
        edge = jnp.where(seen_edge, jnp.where(lower, score(own_ref), score(two_ref)), hidden)
        one = jnp.where(seen_one, score(one_ref), hidden)
        highest = jnp.max(jnp.maximum(edge, one), axis=0, keepdims=True)
        edge = jnp.exp2((edge - highest) * factor)
        one = jnp.exp2((one - highest) * factor)
        inverse = 1.0 / jnp.sum(edge + one, axis=0, keepdims=True)
        edge = edge * inverse
        weights = jnp.concatenate(
            [
                jnp.where(lower, edge, 0.0).astype(jnp.bfloat16),
                (one * inverse).astype(jnp.bfloat16),
                jnp.where(lower, 0.0, edge).astype(jnp.bfloat16),
            ],
            axis=0,
        )
        mixed = jnp.dot(
            jnp.concatenate(turned, axis=1), weights, preferred_element_type=jnp.float32
        )
        for j in range(GROUP):
            head = mixed[:, j * HEAD_SIZE : (j + 1) * HEAD_SIZE]
            if other == 0:
                slab_ref[z2, :, j * HEAD_SIZE : (j + 1) * HEAD_SIZE] = head.T.astype(jnp.bfloat16)
            low, high = head[:HALF], head[HALF:]
            row = (z2 * 8 + j) * HALF
            shift = other * ROWS
            mine_ref[row : row + HALF, :] = jnp.where(core == 0, low, high).astype(jnp.bfloat16)
            theirs_ref[shift + row : shift + row + HALF, :] = jnp.where(
                core == 0, high, low
            ).astype(jnp.bfloat16)
        if other == 0:
            leave(z, z2)
    for copy in leaving:
        copy.wait()


def attention(other, q, own, one, two, *away):
    vmem = pl.BlockSpec(memory_space=pltpu.VMEM)
    hbm = pl.BlockSpec(memory_space=pltpu.HBM)
    shapes = [(2 * ROWS, TOKENS), (16, TOKENS)]
    if other == 0:
        shapes = [(TOKENS, QUERY_HEADS * HEAD_SIZE), (ROWS, TOKENS), (ROWS, TOKENS)]
    return pl.pallas_call(
        functools.partial(attention_kernel, other),
        out_shape=[jax.ShapeDtypeStruct(shape, jnp.bfloat16) for shape in shapes],
        in_specs=[vmem] * (4 + len(away)),
        out_specs=[vmem, vmem] if other else [hbm, vmem, vmem],
        scratch_shapes=()
        if other
        else [
            pltpu.VMEM((4, TOKENS, GROUP * HEAD_SIZE), jnp.bfloat16),
            pltpu.SemaphoreType.DMA((4,)),
        ],
        compiler_params=pltpu.CompilerParams(vmem_limit_bytes=VMEM_LIMIT),
        cost_estimate=pl.CostEstimate(
            flops=1 << 20, bytes_accessed=1 << 18, transcendentals=1 << 10
        )
        if other
        else pl.CostEstimate(flops=3 << 30, bytes_accessed=2 << 20, transcendentals=1 << 19),
    )(q, own, one, two, *away)


def outer_kernel(second_ref, keep_ref, near_ref, far_ref, farthest_ref, out_ref, coeffs_ref):
    pair = 2 * TOKENS

    @pl.when(pl.program_id(0) == 0)
    def _():
        for p in range(MEMBERS // 2):
            part = second_ref[:, :, p * pair : (p + 1) * pair].astype(jnp.float32)
            coeffs_ref[p] = part.reshape(R, pair).astype(jnp.bfloat16)

    total = jnp.zeros(out_ref.shape, jnp.float32)
    for p, refs in enumerate(((keep_ref, near_ref), (far_ref, farthest_ref))):
        total += lax.dot_general(
            jnp.concatenate([ref[...] for ref in refs], axis=1),
            coeffs_ref[p],
            NT,
            preferred_element_type=jnp.float32,
        )
    out_ref[...] = total.astype(jnp.bfloat16)


def outer(second, keep, near, far, farthest):
    step = ROWS // 2
    block = lambda first: pl.BlockSpec((step, TOKENS), lambda i: (i + first, 0))
    return pl.pallas_call(
        outer_kernel,
        out_shape=jax.ShapeDtypeStruct((ROWS, R), jnp.bfloat16),
        grid=(ROWS // step,),
        in_specs=[
            pl.BlockSpec(second.shape, lambda i: (0, 0, 0)),
            block(0),
            block(0),
            block(0),
            block(ROWS // step),
        ],
        out_specs=pl.BlockSpec((step, R), lambda i: (i, 0)),
        scratch_shapes=[pltpu.VMEM((MEMBERS // 2, R, 2 * TOKENS), jnp.bfloat16)],
        compiler_params=pltpu.CompilerParams(vmem_limit_bytes=VMEM_LIMIT),
    )(second, keep, near, far, farthest)


PIECES = (SEQ, 4, TOKENS)


def pack_kernel(
    dest_hbm,
    keys_hbm,
    values_hbm,
    tag_hbm,
    coeffs_hbm,
    basis_hbm,
    own_ref,
    out_ref,
    dest_ref,
    tag_ref,
    coeffs_ref,
    basis_ref,
    sems,
):
    f32, bf16 = jnp.float32, jnp.bfloat16
    pairs = (
        (tag_hbm, tag_ref),
        (coeffs_hbm, coeffs_ref),
        (basis_hbm, basis_ref),
        (keys_hbm, own_ref.at[:, :KV]),
        (values_hbm, own_ref.at[:, KV : 2 * KV]),
        (dest_hbm, dest_ref),
    )
    copies = [pltpu.make_async_copy(a, b, sems.at[i]) for i, (a, b) in enumerate(pairs)]
    for copy in copies:
        copy.start()
    copies[0].wait()
    tags = jnp.broadcast_to(tag_ref[...].astype(f32), (TOKENS, TOKENS)).T + 1.0
    own_ref[:, 2 * KV :] = tags.astype(bf16)
    copies[1].wait()
    out_ref[:, :, :TOKENS] = coeffs_ref[...].astype(f32).T.reshape(PIECES).astype(bf16)
    copies[2].wait()
    count = R // REP
    mine = basis_ref[pl.ds(pl.multiple_of(lax.axis_index("rep") * count, count), count), :]
    gram = lax.dot_general(mine, basis_ref[...], NT, preferred_element_type=f32)
    gram = jnp.concatenate([gram[:, :TOKENS], gram[:, TOKENS:]], axis=0).astype(bf16)
    row = lax.broadcasted_iota(jnp.int32, (R, SEQ), 0)
    column = lax.broadcasted_iota(jnp.int32, (R, SEQ), 1)
    spread = jnp.where(row == column * 4, 1.0, 0.0).astype(bf16)
    extra = jnp.dot(spread, gram, preferred_element_type=f32)
    row = lax.broadcasted_iota(jnp.int32, (R, TOKENS), 0)
    copies[5].wait()
    extra = jnp.where(row % 4 == 0, extra, dest_ref[0, 0].astype(f32))
    out_ref[:, :, TOKENS:] = extra.reshape(PIECES).astype(bf16)
    copies[3].wait()
    copies[4].wait()


def pack(dest, keys, values, tag, coeffs, basis):
    vmem = pl.BlockSpec(memory_space=pltpu.VMEM)
    hbm = pl.BlockSpec(memory_space=pltpu.HBM)
    return pl.pallas_call(
        pack_kernel,
        out_shape=(
            jax.ShapeDtypeStruct((TOKENS, 2 * KV + TOKENS), jnp.bfloat16),
            jax.ShapeDtypeStruct((SEQ, 4, 2 * TOKENS), jnp.bfloat16),
        ),
        in_specs=[hbm] * 6,
        out_specs=(vmem, vmem),
        scratch_shapes=[
            pltpu.SMEM(dest.shape, dest.dtype),
            pltpu.VMEM(tag.shape, tag.dtype),
            pltpu.VMEM(coeffs.shape, coeffs.dtype),
            pltpu.VMEM(basis.shape, basis.dtype),
            pltpu.SemaphoreType.DMA((6,)),
        ],
        compiler_params=pltpu.CompilerParams(vmem_limit_bytes=PACK_VMEM_LIMIT),
    )(dest, keys, values, tag, coeffs, basis)


def sort_kernel(first_ref, mark_ref, out_ref):
    f32, bf16 = jnp.float32, jnp.bfloat16
    pieces = first_ref[:, :, :TOKENS].astype(f32).reshape(R, TOKENS).astype(bf16)
    extra = first_ref[:, :, TOKENS:].astype(f32).reshape(R, TOKENS)
    row = lax.broadcasted_iota(jnp.int32, (R, TOKENS), 0)
    gram = jnp.sum(jnp.where(row % 4 == 0, extra, 0.0), axis=0, keepdims=True)
    dest = jnp.where(row % 4 == 0, pltpu.roll(extra, R - 1, 0), extra)
    dest = jnp.concatenate([dest.T] * 2, axis=0)
    row = lax.broadcasted_iota(jnp.int32, (R, R), 0)
    column = lax.broadcasted_iota(jnp.int32, (R, R), 1)
    same = row % 4 == column % 4
    for m, partner in enumerate(PARTNERS):
        holder = ((row // 4) ^ partner).astype(f32)
        chosen = jnp.where(same & (dest == holder), 1.0, 0.0).astype(bf16)
        sorted_pieces = jnp.dot(chosen, pieces, preferred_element_type=f32)
        out_ref[:, :, m * TOKENS : (m + 1) * TOKENS] = sorted_pieces.reshape(PIECES).astype(bf16)
    out_ref[:, :, MEMBERS * TOKENS :] = jnp.broadcast_to(gram.reshape(1, 1, TOKENS), PIECES).astype(
        bf16
    )


def sort(first, mark):
    vmem = pl.BlockSpec(memory_space=pltpu.VMEM)
    return pl.pallas_call(
        sort_kernel,
        out_shape=jax.ShapeDtypeStruct((SEQ, 4, (MEMBERS + 1) * TOKENS), jnp.bfloat16),
        in_specs=[vmem, vmem],
        out_specs=vmem,
        compiler_params=pltpu.CompilerParams(vmem_limit_bytes=VMEM_LIMIT),
    )(first, mark)


def local(queries, keys, values, doc_ids, coeffs, shard_dest, basis):
    bf16 = jnp.bfloat16

    own, packed = pack(shard_dest, keys[0], values[0], doc_ids, coeffs[0], basis)
    two = shifted(own, 2)
    one = shifted(own, 1)
    first = exchange(packed, "seq")

    away, mark = attention(1, queries[0], own, one, two)
    far = swapped(away, 16)

    second = exchange(sort(first, mark), "seq")
    attended, keep, near = attention(0, queries[0], own, one, two, away)
    near, far = lax.optimization_barrier((near, far))
    near = swapped(near, 1)
    farthest = swapped(far, 1)

    partial = outer(second, keep, near, far, farthest).reshape(SHARES, HALF, R)
    arrived = exchange(partial, "seq", SIXTEENS)
    rows = jnp.sum(arrived.astype(jnp.float32), axis=0).astype(bf16)
    gram_rows = R // REP
    gram_share = second[:, 0, MEMBERS * TOKENS :]
    gram_share = jnp.concatenate([gram_share[:gram_rows], gram_share[gram_rows:]], axis=1)
    last = exchange(
        jnp.broadcast_to(jnp.concatenate([rows, gram_share], axis=0), (REP, HALF + gram_rows, R)),
        "rep",
    )
    summed = jnp.sum(last[:, :HALF].astype(jnp.float32), axis=0)
    gram_all = last[:, HALF:].reshape(R, R).astype(jnp.float32)
    grad = jnp.dot(summed, gram_all, precision=lax.Precision.HIGHEST)
    grad = grad * (1.0 / math.sqrt(REP * SEQ * TOKENS))
    return attended[None], grad


def solution(mesh):
    in_specs = (
        P("rep", "seq", None),
        P("rep", "seq", None),
        P("rep", "seq", None),
        P("rep", "seq"),
        P("rep", "seq", None),
        P("rep", "seq"),
        P(None, "seq"),
    )
    out_specs = (P("rep", "seq", None), P("seq", None))
    return jax.shard_map(local, mesh=mesh, in_specs=in_specs, out_specs=out_specs, check_vma=False)
```

```python
import functools
import math

import jax
import jax.numpy as jnp
from jax import lax
from jax.experimental import pallas as pl
from jax.experimental.pallas import tpu as pltpu
from jax.sharding import PartitionSpec as P

QUERY_HEADS = 32
KEY_VALUE_HEADS = 4
HEAD_SIZE = 128
GROUP = QUERY_HEADS // KEY_VALUE_HEADS
KV = KEY_VALUE_HEADS * HEAD_SIZE
TOKENS = 128
R = 256
SEQ = 64
REP = 8
HALF = HEAD_SIZE // 2
LOG2E = math.log2(math.e)
VMEM_LIMIT = 48 * 1024 * 1024
PACK_VMEM_LIMIT = 66000000
NT = (((1,), (1,)), ((), ()))

PARTNERS = (0, 1, 16, 17)
MEMBERS = len(PARTNERS)
SHARES = SEQ // MEMBERS
ROWS = SHARES * HALF
SIXTEENS = [
    [z2 * 32 + zp * 16 + y * 2 + c for z2 in range(2) for y in range(8)]
    for zp in range(2)
    for c in range(2)
]


def shifted(block, distance):
    return lax.ppermute(block, "seq", [(i, i + distance) for i in range(SEQ - distance)])


def swapped(block, partner):
    return lax.ppermute(block, "seq", [(i, i ^ partner) for i in range(SEQ)])


def exchange(block, axis, groups=None):
    return lax.all_to_all(
        block, axis, split_axis=0, concat_axis=0, axis_index_groups=groups, tiled=True
    )


def attention_kernel(other, q_ref, own_ref, one_ref, two_ref, *refs):
    if other == 0:
        away_ref, out_hbm, mine_ref, theirs_ref, slab_ref, sems = refs
    else:
        mine_ref, mark_ref = refs
        theirs_ref = mine_ref
        mark_ref[...] = jnp.zeros(mark_ref.shape, mark_ref.dtype)
    leaving = []
    seq = lax.axis_index("seq")
    core, odd = seq & 1, (seq >> 4) & 1
    span = GROUP * HEAD_SIZE

    def leave(z, at):
        slab = pl.ds(pl.multiple_of(z * span, span), span)
        leaving.append(pltpu.make_async_copy(slab_ref.at[at], out_hbm.at[:, slab], sems.at[at]))
        leaving[-1].start()

    if other == 0:
        for z2 in range(2):
            for j in range(GROUP):
                row = (z2 * 8 + j) * HALF
                mine = away_ref[row : row + HALF, :].astype(jnp.float32)
                theirs = away_ref[ROWS + row : ROWS + row + HALF, :].astype(jnp.float32)
                head = jnp.concatenate(
                    [jnp.where(core == 0, mine, theirs), jnp.where(core == 0, theirs, mine)], axis=0
                )
                slab_ref[2 + z2, :, j * HEAD_SIZE : (j + 1) * HEAD_SIZE] = head.T.astype(
                    jnp.bfloat16
                )
            leave(z2 * 2 + 1 - odd, 2 + z2)
    square = (TOKENS, TOKENS)
    lower = lax.broadcasted_iota(jnp.int32, square, 0) <= lax.broadcasted_iota(jnp.int32, square, 1)
    tags = lambda block: block[:, 2 * KV :].astype(jnp.float32)
    query_tags = tags(own_ref).T
    wide = lambda mask: jnp.concatenate([mask] * GROUP, axis=1)
    seen_edge = wide(jnp.where(lower, tags(own_ref), tags(two_ref)) == query_tags)
    seen_one = wide(tags(one_ref) == query_tags)
    lower = wide(lower)
    hidden = jnp.float32(-1e30)
    factor = HEAD_SIZE ** (-0.5) * LOG2E
    column = lambda start: pl.ds(pl.multiple_of(start, HEAD_SIZE), HEAD_SIZE)
    for z2 in range(2):
        z = z2 * 2 + (odd if other == 0 else 1 - odd)
        at = z * HEAD_SIZE
        turned = [
            b[:, column(KV + at)].astype(jnp.float32).T.astype(jnp.bfloat16)
            for b in (own_ref, one_ref, two_ref)
        ]
        heads = [(z * GROUP + j) * HEAD_SIZE for j in range(GROUP)]
        q = jnp.concatenate([q_ref[:, column(h)] for h in heads], axis=0)
        score = lambda b: lax.dot_general(
            b[:, column(at)], q, NT, preferred_element_type=jnp.float32
        )
        edge = jnp.where(seen_edge, jnp.where(lower, score(own_ref), score(two_ref)), hidden)
        one = jnp.where(seen_one, score(one_ref), hidden)
        highest = jnp.max(jnp.maximum(edge, one), axis=0, keepdims=True)
        edge = jnp.exp2((edge - highest) * factor)
        one = jnp.exp2((one - highest) * factor)
        inverse = 1.0 / jnp.sum(edge + one, axis=0, keepdims=True)
        edge = edge * inverse
        weights = jnp.concatenate(
            [
                jnp.where(lower, edge, 0.0).astype(jnp.bfloat16),
                (one * inverse).astype(jnp.bfloat16),
                jnp.where(lower, 0.0, edge).astype(jnp.bfloat16),
            ],
            axis=0,
        )
        mixed = jnp.dot(
            jnp.concatenate(turned, axis=1), weights, preferred_element_type=jnp.float32
        )
        for j in range(GROUP):
            head = mixed[:, j * HEAD_SIZE : (j + 1) * HEAD_SIZE]
            if other == 0:
                slab_ref[z2, :, j * HEAD_SIZE : (j + 1) * HEAD_SIZE] = head.T.astype(jnp.bfloat16)
            low, high = head[:HALF], head[HALF:]
            row = (z2 * 8 + j) * HALF
            shift = other * ROWS
            mine_ref[row : row + HALF, :] = jnp.where(core == 0, low, high).astype(jnp.bfloat16)
            theirs_ref[shift + row : shift + row + HALF, :] = jnp.where(
                core == 0, high, low
            ).astype(jnp.bfloat16)
        if other == 0:
            leave(z, z2)
    for copy in leaving:
        copy.wait()


def attention(other, q, own, one, two, *away):
    vmem = pl.BlockSpec(memory_space=pltpu.VMEM)
    hbm = pl.BlockSpec(memory_space=pltpu.HBM)
    shapes = [(2 * ROWS, TOKENS), (16, TOKENS)]
    if other == 0:
        shapes = [(TOKENS, QUERY_HEADS * HEAD_SIZE), (ROWS, TOKENS), (ROWS, TOKENS)]
    return pl.pallas_call(
        functools.partial(attention_kernel, other),
        out_shape=[jax.ShapeDtypeStruct(shape, jnp.bfloat16) for shape in shapes],
        in_specs=[vmem] * (4 + len(away)),
        out_specs=[vmem, vmem] if other else [hbm, vmem, vmem],
        scratch_shapes=()
        if other
        else [
            pltpu.VMEM((4, TOKENS, GROUP * HEAD_SIZE), jnp.bfloat16),
            pltpu.SemaphoreType.DMA((4,)),
        ],
        compiler_params=pltpu.CompilerParams(vmem_limit_bytes=VMEM_LIMIT),
        cost_estimate=pl.CostEstimate(
            flops=1 << 20, bytes_accessed=1 << 18, transcendentals=1 << 10
        )
        if other
        else pl.CostEstimate(flops=3 << 30, bytes_accessed=2 << 20, transcendentals=1 << 19),
    )(q, own, one, two, *away)


def outer_kernel(second_ref, keep_ref, near_ref, far_ref, farthest_ref, out_ref, coeffs_ref):
    pair = 2 * TOKENS

    @pl.when(pl.program_id(0) == 0)
    def _():
        for p in range(MEMBERS // 2):
            part = second_ref[:, :, p * pair : (p + 1) * pair].astype(jnp.float32)
            coeffs_ref[p] = part.reshape(R, pair).astype(jnp.bfloat16)

    total = jnp.zeros(out_ref.shape, jnp.float32)
    for p, refs in enumerate(((keep_ref, near_ref), (far_ref, farthest_ref))):
        total += lax.dot_general(
            jnp.concatenate([ref[...] for ref in refs], axis=1),
            coeffs_ref[p],
            NT,
            preferred_element_type=jnp.float32,
        )
    out_ref[...] = total.astype(jnp.bfloat16)


def outer(second, keep, near, far, farthest):
    step = ROWS
    block = lambda first: pl.BlockSpec((step, TOKENS), lambda i: (i + first, 0))
    return pl.pallas_call(
        outer_kernel,
        out_shape=jax.ShapeDtypeStruct((ROWS, R), jnp.bfloat16),
        grid=(ROWS // step,),
        in_specs=[
            pl.BlockSpec(second.shape, lambda i: (0, 0, 0)),
            block(0),
            block(0),
            block(0),
            block(ROWS // step),
        ],
        out_specs=pl.BlockSpec((step, R), lambda i: (i, 0)),
        scratch_shapes=[pltpu.VMEM((MEMBERS // 2, R, 2 * TOKENS), jnp.bfloat16)],
        compiler_params=pltpu.CompilerParams(vmem_limit_bytes=VMEM_LIMIT),
    )(second, keep, near, far, farthest)


PIECES = (SEQ, 4, TOKENS)


def pack_kernel(
    dest_hbm,
    keys_hbm,
    values_hbm,
    tag_hbm,
    coeffs_hbm,
    basis_hbm,
    own_ref,
    out_ref,
    dest_ref,
    tag_ref,
    coeffs_ref,
    basis_ref,
    sems,
):
    f32, bf16 = jnp.float32, jnp.bfloat16
    pairs = (
        (tag_hbm, tag_ref),
        (coeffs_hbm, coeffs_ref),
        (basis_hbm, basis_ref),
        (keys_hbm, own_ref.at[:, :KV]),
        (values_hbm, own_ref.at[:, KV : 2 * KV]),
        (dest_hbm, dest_ref),
    )
    copies = [pltpu.make_async_copy(a, b, sems.at[i]) for i, (a, b) in enumerate(pairs)]
    for copy in copies:
        copy.start()
    copies[0].wait()
    tags = jnp.broadcast_to(tag_ref[...].astype(f32), (TOKENS, TOKENS)).T + 1.0
    own_ref[:, 2 * KV :] = tags.astype(bf16)
    copies[1].wait()
    out_ref[:, :, :TOKENS] = coeffs_ref[...].astype(f32).T.reshape(PIECES).astype(bf16)
    copies[2].wait()
    count = R // REP
    mine = basis_ref[pl.ds(pl.multiple_of(lax.axis_index("rep") * count, count), count), :]
    gram = lax.dot_general(mine, basis_ref[...], NT, preferred_element_type=f32)
    gram = jnp.concatenate([gram[:, :TOKENS], gram[:, TOKENS:]], axis=0).astype(bf16)
    row = lax.broadcasted_iota(jnp.int32, (R, SEQ), 0)
    column = lax.broadcasted_iota(jnp.int32, (R, SEQ), 1)
    spread = jnp.where(row == column * 4, 1.0, 0.0).astype(bf16)
    extra = jnp.dot(spread, gram, preferred_element_type=f32)
    row = lax.broadcasted_iota(jnp.int32, (R, TOKENS), 0)
    copies[5].wait()
    extra = jnp.where(row % 4 == 0, extra, dest_ref[0, 0].astype(f32))
    out_ref[:, :, TOKENS:] = extra.reshape(PIECES).astype(bf16)
    copies[3].wait()
    copies[4].wait()


def pack(dest, keys, values, tag, coeffs, basis):
    vmem = pl.BlockSpec(memory_space=pltpu.VMEM)
    hbm = pl.BlockSpec(memory_space=pltpu.HBM)
    return pl.pallas_call(
        pack_kernel,
        out_shape=(
            jax.ShapeDtypeStruct((TOKENS, 2 * KV + TOKENS), jnp.bfloat16),
            jax.ShapeDtypeStruct((SEQ, 4, 2 * TOKENS), jnp.bfloat16),
        ),
        in_specs=[hbm] * 6,
        out_specs=(vmem, vmem),
        scratch_shapes=[
            pltpu.SMEM(dest.shape, dest.dtype),
            pltpu.VMEM(tag.shape, tag.dtype),
            pltpu.VMEM(coeffs.shape, coeffs.dtype),
            pltpu.VMEM(basis.shape, basis.dtype),
            pltpu.SemaphoreType.DMA((6,)),
        ],
        compiler_params=pltpu.CompilerParams(vmem_limit_bytes=PACK_VMEM_LIMIT),
    )(dest, keys, values, tag, coeffs, basis)


def sort_kernel(first_ref, mark_ref, out_ref):
    f32, bf16 = jnp.float32, jnp.bfloat16
    pieces = first_ref[:, :, :TOKENS].astype(f32).reshape(R, TOKENS).astype(bf16)
    extra = first_ref[:, :, TOKENS:].astype(f32).reshape(R, TOKENS)
    row = lax.broadcasted_iota(jnp.int32, (R, TOKENS), 0)
    gram = jnp.sum(jnp.where(row % 4 == 0, extra, 0.0), axis=0, keepdims=True)
    dest = jnp.where(row % 4 == 0, pltpu.roll(extra, R - 1, 0), extra)
    dest = jnp.concatenate([dest.T] * 2, axis=0)
    row = lax.broadcasted_iota(jnp.int32, (R, R), 0)
    column = lax.broadcasted_iota(jnp.int32, (R, R), 1)
    same = row % 4 == column % 4
    for m, partner in enumerate(PARTNERS):
        holder = ((row // 4) ^ partner).astype(f32)
        chosen = jnp.where(same & (dest == holder), 1.0, 0.0).astype(bf16)
        sorted_pieces = jnp.dot(chosen, pieces, preferred_element_type=f32)
        out_ref[:, :, m * TOKENS : (m + 1) * TOKENS] = sorted_pieces.reshape(PIECES).astype(bf16)
    out_ref[:, :, MEMBERS * TOKENS :] = jnp.broadcast_to(gram.reshape(1, 1, TOKENS), PIECES).astype(
        bf16
    )


def sort(first, mark):
    vmem = pl.BlockSpec(memory_space=pltpu.VMEM)
    return pl.pallas_call(
        sort_kernel,
        out_shape=jax.ShapeDtypeStruct((SEQ, 4, (MEMBERS + 1) * TOKENS), jnp.bfloat16),
        in_specs=[vmem, vmem],
        out_specs=vmem,
        compiler_params=pltpu.CompilerParams(vmem_limit_bytes=VMEM_LIMIT),
    )(first, mark)


def local(queries, keys, values, doc_ids, coeffs, shard_dest, basis):
    bf16 = jnp.bfloat16

    own, packed = pack(shard_dest, keys[0], values[0], doc_ids, coeffs[0], basis)
    two = shifted(own, 2)
    one = shifted(own, 1)
    first = exchange(packed, "seq")

    away, mark = attention(1, queries[0], own, one, two)
    far = swapped(away, 16)

    second = exchange(sort(first, mark), "seq")
    attended, keep, near = attention(0, queries[0], own, one, two, away)
    near, far = lax.optimization_barrier((near, far))
    near = swapped(near, 1)
    farthest = swapped(far, 1)

    partial = outer(second, keep, near, far, farthest).reshape(SHARES, HALF, R)
    arrived = exchange(partial, "seq", SIXTEENS)
    rows = jnp.sum(arrived.astype(jnp.float32), axis=0).astype(bf16)
    gram_rows = R // REP
    gram_share = second[:, 0, MEMBERS * TOKENS :]
    gram_share = jnp.concatenate([gram_share[:gram_rows], gram_share[gram_rows:]], axis=1)
    last = exchange(
        jnp.broadcast_to(jnp.concatenate([rows, gram_share], axis=0), (REP, HALF + gram_rows, R)),
        "rep",
    )
    summed = jnp.sum(last[:, :HALF].astype(jnp.float32), axis=0)
    gram_all = last[:, HALF:].reshape(R, R).astype(jnp.float32)
    grad = jnp.dot(summed, gram_all, precision=lax.Precision.HIGHEST)
    grad = grad * (1.0 / math.sqrt(REP * SEQ * TOKENS))
    return attended[None], grad


def solution(mesh):
    in_specs = (
        P("rep", "seq", None),
        P("rep", "seq", None),
        P("rep", "seq", None),
        P("rep", "seq"),
        P("rep", "seq", None),
        P("rep", "seq"),
        P(None, "seq"),
    )
    out_specs = (P("rep", "seq", None), P("seq", None))
    return jax.shard_map(local, mesh=mesh, in_specs=in_specs, out_specs=out_specs, check_vma=False)
```
